256 devices in a mesh: row: 8 (over x, core), col: 32 (over z, y).
Axes of the slice: x: 4, y: 4, z: 8, core: 2. Of those that a mesh axis runs over, the one named last changes fastest.
Arguments:
- tokens: bfloat16 [1024, 4096], P('row', 'col'), may hold values from -6 to 6
- gate_weight: bfloat16 [4096, 16384], P('row', 'col'), may hold values from -0.09375 to 0.09375
- up_weight: bfloat16 [4096, 16384], P('row', 'col'), may hold values from -0.09375 to 0.09375
- down_weight: bfloat16 [16384, 4096], P('row', 'col'), may hold values from -0.046875 to 0.046875
- out_grad: bfloat16 [1024, 4096], P('row', 'col'), may hold values from -6 to 6
Outputs:
- output: bfloat16 [1024, 4096], P('row', 'col')
- token_grad: bfloat16 [1024, 4096], P('row', 'col')
- gate_grad: bfloat16 [4096, 16384], P('row', 'col')
- up_grad: bfloat16 [4096, 16384], P('row', 'col')
- down_grad: bfloat16 [16384, 4096], P('row', 'col')
The draws below stay inside these ranges and needn't reach their ends.
All inputs are finite; a program needn't handle non-finite values.
Results may differ from the reference program's by a relative error of at most 0.005.
Values may be sent and summed in bfloat16 or wider, within the bound.
A program may use at most 128 MiB of HBM per device.

```python
import jax
import jax.numpy as jnp
from jax import lax

D = 4096
FF = 16384
TOKENS = 1024


def levels(own_key, shape, split, low, top_value):
    def one(dim, shards_of):
        heights = jax.random.uniform(jax.random.fold_in(jax.random.fold_in(own_key, 6), dim), (shards_of,), jnp.float32, low / len(split), top_value / len(split))
        return jnp.repeat(jnp.exp(heights), shape[dim] // shards_of).reshape((-1,) + (1,) * (len(shape) - dim - 1))

    factor_of = one(*split[0])
    for cut in split[1:]:
        factor_of = factor_of * one(*cut)
    return factor_of


def scatter_about(rng, extent, spread, most, pieces=(), held_as=jnp.bfloat16):
    gain = levels(rng, extent, pieces, -0.22, 0.18) if pieces else 1.0
    drawn = jax.random.normal(rng, extent, jnp.float32) * spread * gain
    return jnp.minimum(jnp.maximum(drawn, -most), most).astype(held_as)


def setup_inputs(seed: int = 0) -> dict:
    key_list = jax.random.split(jax.random.key(seed), 6)
    return {
        "tokens": scatter_about(key_list[0], (TOKENS, D), 1.0, 6.0, ((0, 8), (1, 32))),
        "gate_weight": scatter_about(key_list[1], (D, FF), D ** -0.5, 0.09375, ((0, 8), (1, 32))),
        "up_weight": scatter_about(key_list[2], (D, FF), D ** -0.5, 0.09375, ((0, 8), (1, 32))),
        "down_weight": scatter_about(key_list[3], (FF, D), FF ** -0.5, 0.046875, ((0, 8), (1, 32))),
        "out_grad": scatter_about(key_list[4], (TOKENS, D), 1.0, 6.0, ((0, 8), (1, 32))),
    }


def tdot(left, right):
    return lax.dot_general(left, right, (((0,), (0,)), ((), ())), preferred_element_type=jnp.float32)


def reference(tokens, gate_weight, up_weight, down_weight, out_grad):
    gate_proj = jnp.dot(tokens, gate_weight, preferred_element_type=jnp.float32)
    up_proj = jnp.dot(tokens, up_weight, preferred_element_type=jnp.float32)
    swish_out = jax.nn.silu(gate_proj)
    hidden = (swish_out * up_proj).astype(jnp.bfloat16)
    output = jnp.dot(hidden, down_weight, preferred_element_type=jnp.float32).astype(jnp.bfloat16)
    grad_hidden = jnp.dot(out_grad, down_weight.T, preferred_element_type=jnp.float32)
    sigmoid_g = jax.nn.sigmoid(gate_proj)
    grad_gate = (grad_hidden * up_proj * sigmoid_g * (1.0 + gate_proj * (1.0 - sigmoid_g))).astype(jnp.bfloat16)
    grad_up = (grad_hidden * swish_out).astype(jnp.bfloat16)
    token_grad = (jnp.dot(grad_gate, gate_weight.T, preferred_element_type=jnp.float32)
                  + jnp.dot(grad_up, up_weight.T, preferred_element_type=jnp.float32)).astype(jnp.bfloat16)
    gate_grad = tdot(tokens, grad_gate).astype(jnp.bfloat16)
    up_grad = tdot(tokens, grad_up).astype(jnp.bfloat16)
    down_grad = tdot(hidden, out_grad).astype(jnp.bfloat16)
    return (output, token_grad, gate_grad, up_grad, down_grad)
```

```python
import functools

import jax
import jax.numpy as jnp
from jax import lax
from jax.experimental import pallas as pl
from jax.experimental.pallas import tpu as pltpu
from jax.sharding import PartitionSpec as P

MESH = pl.DeviceIdType.MESH
BF = jnp.bfloat16
F32 = jnp.float32


def nn(a, b):
    return lax.dot_general(a, b, (((1,), (0,)), ((), ())), preferred_element_type=F32)


def nt(a, b):
    return lax.dot_general(a, b, (((1,), (1,)), ((), ())), preferred_element_type=F32)


def tn(a, b):
    return lax.dot_general(a, b, (((0,), (0,)), ((), ())), preferred_element_type=F32)


def kernel(
    dims,
    tok, cot, gate_hbm, up_hbm, down,
    out_o, tg_o, gg_o, ug_o, dg_o,
    xg, gw, dp, hid,
    acc_a, ms_a, mr_a, xs_a, xr_a,
    acc_b, ms_b, mr_b, xs_b, xr_b,
    o32, os, oown, yr, zs, zr, zown, fs, dgs,
    t1s, t1r, tds, tdr, rgs, rgr,
    mas, mar, mbs, mbr, xas, xar, xbs, xbr,
    axs, axr, ams, amr, ysm, yrm, zsm, zrm, f_s, f_r, d_s, d_r, lsem,
):
    nx, ny, nz = dims
    nr = 2 * nx
    tb, dc = tok.shape
    db, fb = gate_hbm.shape
    half = nz // 2

    row, col = lax.axis_index("row"), lax.axis_index("col")
    x, kap = lax.div(row, 2), lax.rem(row, 2)
    z, y = lax.div(col, ny), lax.rem(col, ny)
    mate = (x * 2 + 1 - kap, col)
    diag = row == z

    def xdev(d):
        return (lax.rem(x + d, nx) * 2 + kap, col)

    def ydev(d):
        return (row, z * ny + lax.rem(y + d, ny))

    def zdev(d):
        return (row, lax.rem(z + d, nz) * ny + y)

    def tdev(k):
        return (z, row * ny + k)

    def rows(t):
        return pl.ds(pl.multiple_of(t * tb, tb), tb)

    def lanes(k):
        return pl.ds(pl.multiple_of(k * dc, dc), dc)

    def rc(src, dst, ss, rs, dev):
        return pltpu.make_async_remote_copy(
            src_ref=src, dst_ref=dst, send_sem=ss, recv_sem=rs,
            device_id=dev, device_id_type=MESH,
        )

    cg = pltpu.make_async_copy(gate_hbm, gw.at[:, pl.ds(0, fb)], lsem.at[0])
    cu = pltpu.make_async_copy(up_hbm, gw.at[:, pl.ds(fb, fb)], lsem.at[1])
    cg.start()
    cu.start()

    bar = pltpu.get_barrier_semaphore()

    def greet(dev):
        pl.semaphore_signal(bar, inc=1, device_id=dev, device_id_type=MESH)

    greet(mate)
    for d in range(1, nx):
        greet(xdev(d))
    for d in range(1, ny):
        greet(ydev(d))
    for d in range(1, nz):
        greet(zdev(d))
    for k in range(ny):
        @pl.when(jnp.logical_not(jnp.logical_and(diag, y == k)))
        def _():
            greet(tdev(k))
    pl.semaphore_wait(bar, 1 + (nx - 1) + (ny - 1) + (nz - 1) + ny - jnp.where(diag, 1, 0))

    def is_self(k):
        return jnp.logical_and(diag, y == k)

    for k in range(ny):
        @pl.when(jnp.logical_not(is_self(k)))
        def _():
            dst = xg.at[rows(row), lanes(y)]
            rc(tok, dst, t1s.at[k, 0], t1r.at[y, 0], tdev(k)).start()
            dst = xg.at[rows(row), lanes(ny + y)]
            rc(cot, dst, t1s.at[k, 1], t1r.at[y, 1], tdev(k)).start()

        @pl.when(is_self(k))
        def _():
            xg[rows(z), lanes(y)] = tok[...]
            xg[rows(z), lanes(ny + y)] = cot[...]

    def frows(k):
        return pl.ds(pl.multiple_of(k * fb, fb), fb)

    for k in range(ny):
        @pl.when(jnp.logical_not(is_self(k)))
        def _():
            rc(down.at[frows(k)], dp.at[:, lanes(y)], tds.at[k], tdr.at[y], tdev(k)).start()

        @pl.when(is_self(k))
        def _():
            dp[:, lanes(y)] = down[frows(k)]

    for k in range(ny):
        @pl.when(jnp.logical_not(is_self(k)))
        def _():
            dst = xg.at[rows(z), lanes(k)]
            rc(dst, dst, t1s.at[k, 0], t1r.at[k, 0], tdev(k)).wait_recv()
            dst = xg.at[rows(z), lanes(ny + k)]
            rc(dst, dst, t1s.at[k, 1], t1r.at[k, 1], tdev(k)).wait_recv()

    cg.wait()
    cu.wait()

    def order(i):
        s = lax.div(i + 1, 2)
        return lax.rem(z + nz + s - 2 * s * lax.rem(i, 2), nz)

    def ring(t, way, s):
        dev = zdev(1) if way == 0 else zdev(nz - 1)
        return rc(xg.at[rows(t)], xg.at[rows(t)], rgs.at[way, s], rgr.at[way, s], dev)

    def ring_half(t, way):
        dev = zdev(1) if way == 0 else zdev(nz - 1)
        ref = xg.at[rows(t), pl.ds(way * db, db)]
        return rc(ref, ref, rgs.at[way, half], rgr.at[way, half], dev)

    def reduce_pair(t, acc, mr, xs, xr, ms_sem, mr_sem, xs_sem, xr_sem):
        xt = lax.div(t, 2)
        ref = mr.at[xt]
        rc(ref, ref, ms_sem.at[xt], mr_sem.at[xt], mate).wait_recv()

        @pl.when(xt == x)
        def _():
            acc[xt] = acc[xt] + mr[xt]

        @pl.when(xt != x)
        def _():
            d = lax.rem(xt - x + nx, nx)
            xs[d] = (acc[xt] + mr[xt]).astype(BF)
            rc(xs.at[d], xr.at[d], xs_sem.at[d], xr_sem.at[d], xdev(d)).start()

    set_a = (acc_a, mr_a, xs_a, xr_a, mas, mar, xas, xar)
    set_b = (acc_b, mr_b, xs_b, xr_b, mbs, mbr, xbs, xbr)

    def give(t, part, acc, ms, mr, s_sem, r_sem):
        xt = lax.div(t, 2)

        @pl.when(lax.rem(t, 2) == kap)
        def _():
            acc[xt] = part

        @pl.when(lax.rem(t, 2) != kap)
        def _():
            ms[xt] = part
            rc(ms.at[xt], mr.at[xt], s_sem.at[xt], r_sem.at[xt], mate).start()

    def step_a(i, carry):
        s = lax.div(i + 1, 2)
        odd = lax.rem(i, 2) == 1
        t = order(i)

        @pl.when(i == 0)
        def _():
            ring(t, 0, 1).start()
            ring(t, 1, 1).start()

        @pl.when(jnp.logical_and(odd, s < half))
        def _():
            ring(t, 0, s).wait_recv()

            @pl.when(s + 1 < half)
            def _():
                ring(t, 0, s + 1).start()

            @pl.when(s + 1 == half)
            def _():
                ring_half(t, 0).start()

        @pl.when(jnp.logical_and(jnp.logical_not(odd), s > 0))
        def _():
            ring(t, 1, s).wait_recv()

            @pl.when(s + 1 < half)
            def _():
                ring(t, 1, s + 1).start()

            @pl.when(s + 1 == half)
            def _():
                ring_half(t, 1).start()

        @pl.when(i == nz - 1)
        def _():
            ring_half(t, 0).wait_recv()
            ring_half(t, 1).wait_recv()

        part = nn(xg[rows(t), pl.ds(0, db)], gw[...])
        give(t, part, acc_a, ms_a, mr_a, mas, mar)

        before = order(jnp.maximum(i - 1, 0))

        @pl.when(jnp.logical_and(i > 0, lax.rem(before, 2) == kap))
        def _():
            reduce_pair(before, *set_a)

        return carry

    lax.fori_loop(0, nz, step_a, 0)

    for k in range(ny):
        @pl.when(jnp.logical_not(is_self(k)))
        def _():
            dst = dp.at[:, lanes(k)]
            rc(dst, dst, tds.at[k], tdr.at[k], tdev(k)).wait_recv()

    def step_b(i, carry):
        t = order(i)
        part = nt(xg[rows(t), pl.ds(db, db)], dp[...])
        give(t, part, acc_b, ms_b, mr_b, mbs, mbr)

        before = order(jnp.maximum(i - 1, 0))

        @pl.when(jnp.logical_and(i == 0, lax.rem(order(nz - 1), 2) == kap))
        def _():
            reduce_pair(order(nz - 1), *set_a)

        @pl.when(jnp.logical_and(i > 0, lax.rem(before, 2) == kap))
        def _():
            reduce_pair(before, *set_b)

        return carry

    lax.fori_loop(0, nz, step_b, 0)

    @pl.when(lax.rem(order(nz - 1), 2) == kap)
    def _():
        reduce_pair(order(nz - 1), *set_b)

    for d in range(1, nx):
        rc(xr_a.at[d], xr_a.at[d], xas.at[d], xar.at[d], xdev(d)).wait_recv()
        rc(xr_b.at[d], xr_b.at[d], xbs.at[d], xbr.at[d], xdev(d)).wait_recv()

    chunk = 16

    def point(i, carry):
        r0 = pl.multiple_of(i * chunk, chunk)
        here = pl.ds(r0, chunk)
        sa = acc_a[x, here, :]
        sb = acc_b[x, here, :]
        for d in range(1, nx):
            sa = sa + xr_a[d, here, :].astype(F32)
            sb = sb + xr_b[d, here, :].astype(F32)
        g, u = sa[:, :fb], sa[:, fb:]
        sig = jax.nn.sigmoid(g)
        sw = g * sig
        there = pl.ds(pl.multiple_of(row * tb + r0, chunk), chunk)
        hid[there, pl.ds(0, fb)] = (sw * u).astype(BF)
        hid[there, pl.ds(fb, fb)] = (sb * u * sig * (1.0 + g * (1.0 - sig))).astype(BF)
        hid[there, pl.ds(2 * fb, fb)] = (sb * sw).astype(BF)
        return carry

    lax.fori_loop(0, tb // chunk, point, 0)

    def hcopy(t, ss, rs, dev):
        return rc(hid.at[rows(t)], hid.at[rows(t)], ss, rs, dev)

    for d in range(1, nx):
        hcopy(row, axs.at[d], axr.at[d], xdev(d)).start()
    hcopy(row, ams.at[0], amr.at[0], mate).start()

    def dist(j):
        q = lax.div(j, 2)
        return jnp.where(lax.rem(q, 2) == 1, lax.div(q + 1, 2), lax.rem(nx - lax.div(q, 2), nx))

    def block(j):
        src = lax.rem(x - dist(j) + nx, nx)
        return src * 2 + jnp.where(lax.rem(j, 2) == 0, kap, 1 - kap)

    def ycopy(t, d):
        return rc(os.at[t, d - 1], yr.at[t, d - 1], ysm.at[t, d - 1], yrm.at[t, d - 1], ydev(d))

    def reduce_y(t):
        total = oown[t]
        for d in range(1, ny):
            ycopy(t, d).wait_recv()
            total = total + yr[t, d - 1].astype(F32)

        @pl.when(t == z)
        def _():
            zown[...] = total

        @pl.when(t != z)
        def _():
            d = lax.rem(t - z + nz, nz)
            zs[d] = total.astype(BF)
            rc(zs.at[d], zr.at[d], zsm.at[d], zrm.at[d], zdev(d)).start()

    def step_c(j, carry):
        t = block(j)
        d = dist(j)
        even = lax.rem(j, 2) == 0

        @pl.when(jnp.logical_and(even, d > 0))
        def _():
            hcopy(t, axs.at[d], axr.at[d], xdev(d)).wait_recv()
            hcopy(t, ams.at[d], amr.at[d], mate).start()

        @pl.when(jnp.logical_not(even))
        def _():
            hcopy(t, ams.at[d], amr.at[d], mate).wait_recv()

        o32[:, pl.ds(0, db)] = nn(hid[rows(t), pl.ds(0, fb)], dp[...])
        o32[:, pl.ds(db, db)] = nt(hid[rows(t), pl.ds(fb, 2 * fb)], gw[...])
        for e in range(1, ny):
            k = lax.rem(y + e, ny)
            os[t, e - 1, :, pl.ds(0, dc)] = o32[:, lanes(k)].astype(BF)
            os[t, e - 1, :, pl.ds(dc, dc)] = o32[:, lanes(ny + k)].astype(BF)
            ycopy(t, e).start()
        oown[t, :, pl.ds(0, dc)] = o32[:, lanes(y)]
        oown[t, :, pl.ds(dc, dc)] = o32[:, lanes(ny + y)]

        @pl.when(j > 0)
        def _():
            reduce_y(block(jnp.maximum(j - 1, 0)))

        return carry

    lax.fori_loop(0, nr, step_c, 0)

    for k in range(ny):
        dgs[k] = tn(hid[:, pl.ds(0, fb)], xg[:, pl.ds(db + k * dc, dc)]).astype(BF)

        @pl.when(jnp.logical_not(is_self(k)))
        def _():
            rc(dgs.at[k], dg_o.at[frows(y)], d_s.at[k], d_r.at[y], tdev(k)).start()

        @pl.when(is_self(k))
        def _():
            dg_o[frows(y)] = dgs[k]

    reduce_y(block(nr - 1))

    for k in range(ny):
        w = tn(xg[:, pl.ds(k * dc, dc)], hid[:, pl.ds(fb, 2 * fb)]).astype(BF)
        gg_o[pl.ds(k * dc, dc)] = w[:, :fb]
        ug_o[pl.ds(k * dc, dc)] = w[:, fb:]

    total = zown[...]
    for d in range(1, nz):
        rc(zr.at[d], zr.at[d], zsm.at[d], zrm.at[d], zdev(d)).wait_recv()
        total = total + zr[d].astype(F32)
    fs[...] = total.astype(BF)

    def fcopy(w):
        dst = out_o if w == 0 else tg_o
        return rc(fs.at[:, pl.ds(w * dc, dc)], dst, f_s.at[w], f_r.at[w], tdev(y))

    @pl.when(diag)
    def _():
        out_o[...] = fs[:, pl.ds(0, dc)]
        tg_o[...] = fs[:, pl.ds(dc, dc)]

    @pl.when(jnp.logical_not(diag))
    def _():
        fcopy(0).start()
        fcopy(1).start()
        fcopy(0).wait_recv()
        fcopy(1).wait_recv()

    for k in range(ny):
        @pl.when(jnp.logical_not(is_self(k)))
        def _():
            rc(dgs.at[k], dg_o.at[frows(k)], d_s.at[k], d_r.at[k], tdev(k)).wait_recv()

    @pl.when(jnp.logical_not(diag))
    def _():
        fcopy(0).wait_send()
        fcopy(1).wait_send()

    for k in range(ny):
        @pl.when(jnp.logical_not(is_self(k)))
        def _():
            rc(tok, tok, t1s.at[k, 0], t1r.at[k, 0], tdev(k)).wait_send()
            rc(cot, cot, t1s.at[k, 1], t1r.at[k, 1], tdev(k)).wait_send()
            rc(down.at[frows(k)], dp.at[:, lanes(y)], tds.at[k], tdr.at[k], tdev(k)).wait_send()
            rc(dgs.at[k], dgs.at[k], d_s.at[k], d_r.at[k], tdev(k)).wait_send()

    for way in range(2):
        for s in range(1, half):
            ring(z, way, s).wait_send()
        ring_half(z, way).wait_send()

    for q in range(nx):
        rc(ms_a.at[q], mr_a.at[q], mas.at[q], mar.at[q], mate).wait_send()
        rc(ms_b.at[q], mr_b.at[q], mbs.at[q], mbr.at[q], mate).wait_send()
        hcopy(row, ams.at[q], amr.at[q], mate).wait_send()
    for d in range(1, nx):
        rc(xs_a.at[d], xr_a.at[d], xas.at[d], xar.at[d], xdev(d)).wait_send()
        rc(xs_b.at[d], xr_b.at[d], xbs.at[d], xbr.at[d], xdev(d)).wait_send()
        hcopy(row, axs.at[d], axr.at[d], xdev(d)).wait_send()
    for d in range(1, nz):
        rc(zs.at[d], zr.at[d], zsm.at[d], zrm.at[d], zdev(d)).wait_send()

    def ydone(t, carry):
        for d in range(1, ny):
            ycopy(t, d).wait_send()
        return carry

    lax.fori_loop(0, nr, ydone, 0)


def local(dims, tokens, gate_weight, up_weight, down_weight, out_grad):
    nx, ny, nz = dims
    nr = 2 * nx
    tb, dc = tokens.shape
    db, fb = gate_weight.shape
    t = nr * tb
    vm = pl.BlockSpec(memory_space=pltpu.VMEM)
    hbm = pl.BlockSpec(memory_space=pl.ANY)
    dma = pltpu.SemaphoreType.DMA
    half = nz // 2

    def pair(width):
        return [
            pltpu.VMEM((nx, tb, width), F32),
            pltpu.VMEM((nx, tb, width), F32),
            pltpu.VMEM((nx, tb, width), F32),
            pltpu.VMEM((nx, tb, width), BF),
            pltpu.VMEM((nx, tb, width), BF),
        ]

    scratch = [
        pltpu.VMEM((t, 2 * db), BF),
        pltpu.VMEM((db, 2 * fb), BF),
        pltpu.VMEM((fb, db), BF),
        pltpu.VMEM((t, 3 * fb), BF),
        *pair(2 * fb),
        *pair(fb),
        pltpu.VMEM((tb, 2 * db), F32),
        pltpu.VMEM((nr, ny - 1, tb, 2 * dc), BF),
        pltpu.VMEM((nr, tb, 2 * dc), F32),
        pltpu.VMEM((nr, ny - 1, tb, 2 * dc), BF),
        pltpu.VMEM((nz, tb, 2 * dc), BF),
        pltpu.VMEM((nz, tb, 2 * dc), BF),
        pltpu.VMEM((tb, 2 * dc), F32),
        pltpu.VMEM((tb, 2 * dc), BF),
        pltpu.VMEM((ny, fb, dc), BF),
        dma((ny, 2)), dma((ny, 2)), dma((ny,)), dma((ny,)),
        dma((2, half + 1)), dma((2, half + 1)),
        *[dma((nx,))] * 8,
        *[dma((nx,))] * 4,
        dma((nr, ny - 1)), dma((nr, ny - 1)), dma((nz,)), dma((nz,)),
        dma((2,)), dma((2,)), dma((ny,)), dma((ny,)), dma((2,)),
    ]
    shape = jax.ShapeDtypeStruct
    return pl.pallas_call(
        functools.partial(kernel, dims),
        out_shape=(
            shape((tb, dc), BF),
            shape((tb, dc), BF),
            shape((db, fb), BF),
            shape((db, fb), BF),
            shape((ny * fb, dc), BF),
        ),
        in_specs=[vm, vm, hbm, hbm, vm],
        out_specs=(vm,) * 5,
        scratch_shapes=scratch,
        compiler_params=pltpu.CompilerParams(
            collective_id=0, has_side_effects=True, vmem_limit_bytes=50 * 2**20
        ),
        name="swiglu",
    )(tokens, out_grad, gate_weight, up_weight, down_weight)


def solution(mesh):
    nr, nc = mesh.shape["row"], mesh.shape["col"]
    dims = (nr // 2, nc // nr, nr)
    spec = P("row", "col")
    return jax.shard_map(
        functools.partial(local, dims),
        mesh=mesh,
        in_specs=(spec,) * 5,
        out_specs=(spec,) * 5,
        check_vma=False,
    )
```

```python
import functools

import jax
import jax.numpy as jnp
from jax import lax
from jax.experimental import pallas as pl
from jax.experimental.pallas import tpu as pltpu
from jax.sharding import PartitionSpec as P

MESH = pl.DeviceIdType.MESH
BF = jnp.bfloat16
F32 = jnp.float32


def nn(a, b):
    return lax.dot_general(a, b, (((1,), (0,)), ((), ())), preferred_element_type=F32)


def nt(a, b):
    return lax.dot_general(a, b, (((1,), (1,)), ((), ())), preferred_element_type=F32)


def tn(a, b):
    return lax.dot_general(a, b, (((0,), (0,)), ((), ())), preferred_element_type=F32)


def kernel(
    dims,
    tok, cot, gate_hbm, up_hbm, down,
    out_o, tg_o, gg_o, ug_o, dg_o,
    xg, gw, dp, hh, hg, mid, mid2,
    acc_a, ms_a, mr_a, xs_a, xr_a,
    acc_b, ms_b, mr_b, xs_b, xr_b,
    o32, os_o, own_o, yr_o, os_t, own_t, yr_t,
    zs, zr, zown, fs, dgs,
    t1s, t1r, tys, tyr, trs, trr, crs, crr, cys, cyr,
    d1s, d1r, d2s, d2r, e1s, e1r, e2s, e2r,
    mas, mar, mbs, mbr, xas, xar, xbs, xbr,
    hxs, hxr, hms, hmr, gxs, gxr, gms, gmr,
    yos, yor, yts, ytr, zsm, zrm, f_s, f_r, lsem,
):
    nx, ny, nz = dims
    nr = 2 * nx
    tb, dc = tok.shape
    db, fb = gate_hbm.shape
    half = nz // 2

    row, col = lax.axis_index("row"), lax.axis_index("col")
    x, kap = lax.div(row, 2), lax.rem(row, 2)
    z, y = lax.div(col, ny), lax.rem(col, ny)
    mate = (x * 2 + 1 - kap, col)
    diag = row == z
    twin = (z, row * ny + y)

    def xdev(d):
        return (lax.rem(x + d, nx) * 2 + kap, col)

    def ydev(d):
        return (row, z * ny + lax.rem(y + d, ny))

    def zdev(d):
        return (row, lax.rem(z + d, nz) * ny + y)

    def leg1_to(k):
        return (lax.rem(x + y - k + 1 + nx, nx) * 2 + kap, z * ny + k)

    def leg1_from(s):
        return (lax.rem(x + y - s - 1 + 2 * nx, nx) * 2 + kap, z * ny + s)

    def leg2_to(s):
        return (z, (lax.rem(x + y - s - 1 + 2 * nx, nx) * 2 + kap) * ny + y)

    def leg2_from(s):
        return (lax.rem(lax.div(z, 2) + s - y + 1 + nx, nx) * 2 + lax.rem(z, 2), row * ny + y)

    def leg2_home(s):
        return jnp.logical_and(diag, lax.rem(x + y - s - 1 + 2 * nx, nx) == x)

    def leg2_kept(s):
        return jnp.logical_and(diag, lax.rem(x + s - y + 1 + nx, nx) == x)

    def rows(t):
        return pl.ds(pl.multiple_of(t * tb, tb), tb)

    def lanes(k):
        return pl.ds(pl.multiple_of(k * dc, dc), dc)

    def frows(k):
        return pl.ds(pl.multiple_of(k * fb, fb), fb)

    def rc(src, dst, ss, rs, dev):
        return pltpu.make_async_remote_copy(
            src_ref=src, dst_ref=dst, send_sem=ss, recv_sem=rs,
            device_id=dev, device_id_type=MESH,
        )

    def no(cond):
        return jnp.logical_not(cond)

    cg = pltpu.make_async_copy(gate_hbm, gw.at[:, pl.ds(0, fb)], lsem.at[0])
    cu = pltpu.make_async_copy(up_hbm, gw.at[:, pl.ds(fb, fb)], lsem.at[1])
    cg.start()
    cu.start()

    bar = pltpu.get_barrier_semaphore()

    def greet(dev):
        pl.semaphore_signal(bar, inc=1, device_id=dev, device_id_type=MESH)

    greet(mate)
    for d in range(1, nx):
        greet(xdev(d))
    for d in range(1, ny):
        greet(ydev(d))
    for d in range(1, nz):
        greet(zdev(d))

    @pl.when(no(diag))
    def _():
        greet(twin)

    count = 1 + (nx - 1) + (ny - 1) + (nz - 1) + 2 * ny + jnp.where(diag, 0, 1)
    for s in range(ny):
        greet(leg1_to(s))
        greet(leg1_from(s))

        @pl.when(no(leg2_home(s)))
        def _():
            greet(leg2_to(s))

        @pl.when(no(leg2_kept(s)))
        def _():
            greet(leg2_from(s))

        count = count + jnp.where(leg2_home(s), 0, 1) + jnp.where(leg2_kept(s), 0, 1)
    pl.semaphore_wait(bar, count)

    def mine(w):
        return lanes(w * ny + y)

    @pl.when(no(diag))
    def _():
        rc(tok, xg.at[rows(row), mine(0)], t1s.at[0], t1r.at[0], twin).start()
        rc(cot, xg.at[rows(row), mine(1)], t1s.at[1], t1r.at[1], twin).start()

    @pl.when(diag)
    def _():
        xg[rows(z), mine(0)] = tok[...]
        xg[rows(z), mine(1)] = cot[...]

    for k in range(ny):
        rc(down.at[frows(k)], mid.at[y], d1s.at[k], d1r.at[y], leg1_to(k)).start()

    def ty(d):
        ref = xg.at[rows(z), mine(0)]
        return rc(ref, ref, tys.at[d], tyr.at[d], ydev(d))

    def tring(t, way, s):
        ref = xg.at[rows(t), pl.ds(0, db)]
        return rc(ref, ref, trs.at[way, s], trr.at[way, s], zdev(1 if way == 0 else nz - 1))

    def tring_half(t, way):
        ref = xg.at[rows(t), pl.ds(way * (db // 2), db // 2)]
        return rc(ref, ref, trs.at[way, half], trr.at[way, half], zdev(1 if way == 0 else nz - 1))

    def cring(t, way, s):
        ref = xg.at[rows(t), mine(1)]
        return rc(ref, ref, crs.at[way, s], crr.at[way, s], zdev(1 if way == 0 else nz - 1))

    def cring_half(t, way):
        ht = tb // 2
        ref = xg.at[pl.ds(pl.multiple_of(t * tb + way * ht, ht), ht), mine(1)]
        return rc(ref, ref, crs.at[way, half], crr.at[way, half], zdev(1 if way == 0 else nz - 1))

    def cy(t, d):
        ref = xg.at[rows(t), mine(1)]
        return rc(ref, ref, cys.at[t, d - 1], cyr.at[t, d - 1], ydev(d))

    @pl.when(no(diag))
    def _():
        ref = xg.at[rows(z), mine(0)]
        rc(ref, ref, t1s.at[0], t1r.at[0], twin).wait_recv()

    for d in range(1, ny):
        ty(d).start()

    @pl.when(no(diag))
    def _():
        ref = xg.at[rows(z), mine(1)]
        rc(ref, ref, t1s.at[1], t1r.at[1], twin).wait_recv()

    cring(z, 0, 1).start()
    cring(z, 1, 1).start()
    for d in range(1, ny):
        cy(z, d).start()

    cg.wait()
    cu.wait()

    for d in range(1, ny):
        ty(d).wait_recv()

    def order(i):
        s = lax.div(i + 1, 2)
        return lax.rem(z + nz + s - 2 * s * lax.rem(i, 2), nz)

    def pass_on(i, full, part):
        s = lax.div(i + 1, 2)
        odd = lax.rem(i, 2) == 1
        t = order(i)
        for way in range(2):
            side = odd if way == 0 else jnp.logical_and(no(odd), s > 0)

            @pl.when(jnp.logical_and(side, s < half))
            def _():
                full(t, way, s).wait_recv()

                @pl.when(s + 1 < half)
                def _():
                    full(t, way, s + 1).start()

                @pl.when(s + 1 == half)
                def _():
                    part(t, way).start()

        @pl.when(i == nz - 1)
        def _():
            part(t, 0).wait_recv()
            part(t, 1).wait_recv()

    def reduce_pair(t, acc, mr, xs, xr, ms_sem, mr_sem, xs_sem, xr_sem):
        xt = lax.div(t, 2)
        ref = mr.at[xt]
        rc(ref, ref, ms_sem.at[xt], mr_sem.at[xt], mate).wait_recv()

        @pl.when(xt == x)
        def _():
            acc[xt] = acc[xt] + mr[xt]

        @pl.when(xt != x)
        def _():
            d = lax.rem(xt - x + nx, nx)
            xs[d] = (acc[xt] + mr[xt]).astype(BF)
            rc(xs.at[d], xr.at[d], xs_sem.at[d], xr_sem.at[d], xdev(d)).start()

    set_a = (acc_a, mr_a, xs_a, xr_a, mas, mar, xas, xar)
    set_b = (acc_b, mr_b, xs_b, xr_b, mbs, mbr, xbs, xbr)

    def give(t, part, acc, ms, mr, s_sem, r_sem):
        xt = lax.div(t, 2)

        @pl.when(lax.rem(t, 2) == kap)
        def _():
            acc[xt] = part

        @pl.when(lax.rem(t, 2) != kap)
        def _():
            ms[xt] = part
            rc(ms.at[xt], mr.at[xt], s_sem.at[xt], r_sem.at[xt], mate).start()

    def leg2(src, dst_of, s1, r1, s2, r2, s):
        ref = src.at[s]
        rc(ref, ref, s1.at[s], r1.at[s], leg1_from(s)).wait_recv()

        @pl.when(no(leg2_home(s)))
        def _():
            rc(ref, dst_of(s), s2.at[s], r2.at[s], leg2_to(s)).start()

        @pl.when(leg2_home(s))
        def _():
            pltpu.make_async_copy(ref, dst_of(s), lsem.at[2]).start()
            pltpu.make_async_copy(ref, dst_of(s), lsem.at[2]).wait()

    def dp_at(s):
        return dp.at[:, lanes(s)]

    def dg_at(s):
        return dg_o.at[frows(s)]

    tring(z, 0, 1).start()
    tring(z, 1, 1).start()

    def step_a(i, carry):
        t = order(i)
        pass_on(i, tring, tring_half)
        part = nn(xg[rows(t), pl.ds(0, db)], gw[...])
        give(t, part, acc_a, ms_a, mr_a, mas, mar)

        before = order(jnp.maximum(i - 1, 0))

        @pl.when(jnp.logical_and(i > 0, lax.rem(before, 2) == kap))
        def _():
            reduce_pair(before, *set_a)

        pass_on(i, cring, cring_half)

        @pl.when(i > 0)
        def _():
            for d in range(1, ny):
                cy(t, d).start()

        @pl.when(i == 1)
        def _():
            for s in range(ny):
                leg2(mid, dp_at, d1s, d1r, d2s, d2r, s)

        return carry

    lax.fori_loop(0, nz, step_a, 0)

    @pl.when(lax.rem(order(nz - 1), 2) == kap)
    def _():
        reduce_pair(order(nz - 1), *set_a)

    for s in range(ny):
        @pl.when(no(leg2_kept(s)))
        def _():
            rc(dp_at(s), dp_at(s), d2s.at[s], d2r.at[s], leg2_from(s)).wait_recv()

    def step_b(i, carry):
        t = order(i)
        for d in range(1, ny):
            ref = xg.at[rows(t), lanes(ny + lax.rem(y - d + ny, ny))]
            rc(ref, ref, cys.at[t, d - 1], cyr.at[t, d - 1], ydev(d)).wait_recv()
        part = nt(xg[rows(t), pl.ds(db, db)], dp[...])
        give(t, part, acc_b, ms_b, mr_b, mbs, mbr)

        before = order(jnp.maximum(i - 1, 0))

        @pl.when(jnp.logical_and(i > 0, lax.rem(before, 2) == kap))
        def _():
            reduce_pair(before, *set_b)

        return carry

    lax.fori_loop(0, nz, step_b, 0)

    @pl.when(lax.rem(order(nz - 1), 2) == kap)
    def _():
        reduce_pair(order(nz - 1), *set_b)

    chunk = 16

    def spot(i):
        r0 = pl.multiple_of(i * chunk, chunk)
        return pl.ds(r0, chunk), pl.ds(pl.multiple_of(row * tb + r0, chunk), chunk)

    for d in range(1, nx):
        rc(xr_a.at[d], xr_a.at[d], xas.at[d], xar.at[d], xdev(d)).wait_recv()

    def point_h(i, carry):
        here, there = spot(i)
        sa = acc_a[x, here, :]
        for d in range(1, nx):
            sa = sa + xr_a[d, here, :].astype(F32)
        acc_a[x, here, :] = sa
        g, u = sa[:, :fb], sa[:, fb:]
        hh[there, :] = (g * jax.nn.sigmoid(g) * u).astype(BF)
        return carry

    lax.fori_loop(0, tb // chunk, point_h, 0)

    def hcopy(buf, t, ss, rs, dev):
        return rc(buf.at[rows(t)], buf.at[rows(t)], ss, rs, dev)

    def share(buf, xs_sem, xr_sem, ms_sem, mr_sem):
        hcopy(buf, row, ms_sem.at[0], mr_sem.at[0], mate).start()
        for d in range(1, nx):
            hcopy(buf, row, xs_sem.at[d], xr_sem.at[d], xdev(d)).start()

    share(hh, hxs, hxr, hms, hmr)

    for d in range(1, nx):
        rc(xr_b.at[d], xr_b.at[d], xbs.at[d], xbr.at[d], xdev(d)).wait_recv()

    def point_g(i, carry):
        here, there = spot(i)
        sa = acc_a[x, here, :]
        sb = acc_b[x, here, :]
        for d in range(1, nx):
            sb = sb + xr_b[d, here, :].astype(F32)
        g, u = sa[:, :fb], sa[:, fb:]
        sig = jax.nn.sigmoid(g)
        hg[there, pl.ds(0, fb)] = (sb * u * sig * (1.0 + g * (1.0 - sig))).astype(BF)
        hg[there, pl.ds(fb, fb)] = (sb * (g * sig)).astype(BF)
        return carry

    lax.fori_loop(0, tb // chunk, point_g, 0)
    share(hg, gxs, gxr, gms, gmr)

    def dist(j):
        q = lax.div(j, 2)
        return jnp.where(lax.rem(q, 2) == 1, lax.div(q + 1, 2), lax.rem(nx - lax.div(q, 2), nx))

    def block(j):
        src = lax.rem(x - dist(j) + nx, nx)
        return src * 2 + jnp.where(lax.rem(j, 2) == 0, kap, 1 - kap)

    def arrive(buf, j, xs_sem, xr_sem, ms_sem, mr_sem):
        t, d = block(j), dist(j)
        even = lax.rem(j, 2) == 0

        @pl.when(jnp.logical_and(even, d > 0))
        def _():
            hcopy(buf, t, xs_sem.at[d], xr_sem.at[d], xdev(d)).wait_recv()
            hcopy(buf, t, ms_sem.at[d], mr_sem.at[d], mate).start()

        @pl.when(no(even))
        def _():
            hcopy(buf, t, ms_sem.at[d], mr_sem.at[d], mate).wait_recv()

    def ycopy(w, t, d):
        os, yr, ss, rs = ((os_o, yr_o, yos, yor), (os_t, yr_t, yts, ytr))[w]
        return rc(os.at[t, d - 1], yr.at[t, d - 1], ss.at[t, d - 1], rs.at[t, d - 1], ydev(d))

    def spread(w, t, part):
        os, own = ((os_o, own_o), (os_t, own_t))[w]
        o32[...] = part
        for e in range(1, ny):
            os[t, e - 1] = o32[:, lanes(lax.rem(y + e, ny))].astype(BF)
            ycopy(w, t, e).start()
        own[t] = o32[:, lanes(y)]

    def zcopy(w, d):
        return rc(zs.at[w, d], zr.at[w, d], zsm.at[w, d], zrm.at[w, d], zdev(d))

    def reduce_y(w, t):
        own, yr = ((own_o, yr_o), (own_t, yr_t))[w]
        total = own[t]
        for d in range(1, ny):
            ycopy(w, t, d).wait_recv()
            total = total + yr[t, d - 1].astype(F32)

        @pl.when(t == z)
        def _():
            zown[w] = total

        @pl.when(t != z)
        def _():
            d = lax.rem(t - z + nz, nz)
            zs[w, d] = total.astype(BF)
            zcopy(w, d).start()

    def step_c(j, carry):
        arrive(hh, j, hxs, hxr, hms, hmr)
        t = block(j)
        spread(0, t, nn(hh[rows(t), :], dp[...]))
        return carry

    lax.fori_loop(0, nr, step_c, 0)

    for k in range(ny):
        dgs[k] = tn(hh[...], xg[:, pl.ds(db + k * dc, dc)]).astype(BF)
        rc(dgs.at[k], mid2.at[y], e1s.at[k], e1r.at[y], leg1_to(k)).start()

    lag = 2

    def step_d(j, carry):
        arrive(hg, j, gxs, gxr, gms, gmr)
        t = block(j)
        spread(1, t, nt(hg[rows(t), :], gw[...]))
        reduce_y(0, t)

        @pl.when(j >= lag)
        def _():
            reduce_y(1, block(jnp.maximum(j - lag, 0)))

        @pl.when(j == nr // 2)
        def _():
            for s in range(ny):
                leg2(mid2, dg_at, e1s, e1r, e2s, e2r, s)

        return carry

    lax.fori_loop(0, nr, step_d, 0)

    for k in range(ny):
        w = tn(xg[:, pl.ds(k * dc, dc)], hg[...]).astype(BF)
        gg_o[pl.ds(k * dc, dc)] = w[:, :fb]
        ug_o[pl.ds(k * dc, dc)] = w[:, fb:]

    for j in range(nr - lag, nr):
        reduce_y(1, block(j))

    def fcopy(w):
        return rc(fs.at[w], (out_o, tg_o)[w], f_s.at[w], f_r.at[w], twin)

    for w in range(2):
        total = zown[w]
        for d in range(1, nz):
            zcopy(w, d).wait_recv()
            total = total + zr[w, d].astype(F32)
        fs[w] = total.astype(BF)

        @pl.when(diag)
        def _():
            (out_o, tg_o)[w][...] = fs[w]

        @pl.when(no(diag))
        def _():
            fcopy(w).start()

    @pl.when(no(diag))
    def _():
        for w in range(2):
            fcopy(w).wait_recv()

    for s in range(ny):
        @pl.when(no(leg2_kept(s)))
        def _():
            rc(dg_at(s), dg_at(s), e2s.at[s], e2r.at[s], leg2_from(s)).wait_recv()

    @pl.when(no(diag))
    def _():
        for w in range(2):
            fcopy(w).wait_send()
        rc(tok, tok, t1s.at[0], t1r.at[0], twin).wait_send()
        rc(cot, cot, t1s.at[1], t1r.at[1], twin).wait_send()

    for k in range(ny):
        rc(dgs.at[k], mid.at[k], d1s.at[k], d1r.at[k], leg1_to(k)).wait_send()
        rc(dgs.at[k], mid.at[k], e1s.at[k], e1r.at[k], leg1_to(k)).wait_send()

        @pl.when(no(leg2_home(k)))
        def _():
            rc(mid.at[k], dp_at(k), d2s.at[k], d2r.at[k], leg2_to(k)).wait_send()
            rc(mid2.at[k], dg_at(k), e2s.at[k], e2r.at[k], leg2_to(k)).wait_send()

    for d in range(1, ny):
        ty(d).wait_send()
    for way in range(2):
        for s in range(1, half):
            tring(z, way, s).wait_send()
            cring(z, way, s).wait_send()
        tring_half(z, way).wait_send()
        cring_half(z, way).wait_send()

    for q in range(nx):
        rc(ms_a.at[q], mr_a.at[q], mas.at[q], mar.at[q], mate).wait_send()
        rc(ms_b.at[q], mr_b.at[q], mbs.at[q], mbr.at[q], mate).wait_send()
        hcopy(hh, row, hms.at[q], hmr.at[q], mate).wait_send()
        hcopy(hg, row, gms.at[q], gmr.at[q], mate).wait_send()
    for d in range(1, nx):
        rc(xs_a.at[d], xr_a.at[d], xas.at[d], xar.at[d], xdev(d)).wait_send()
        rc(xs_b.at[d], xr_b.at[d], xbs.at[d], xbr.at[d], xdev(d)).wait_send()
        hcopy(hh, row, hxs.at[d], hxr.at[d], xdev(d)).wait_send()
        hcopy(hg, row, gxs.at[d], gxr.at[d], xdev(d)).wait_send()
    for d in range(1, nz):
        zcopy(0, d).wait_send()
        zcopy(1, d).wait_send()

    def ydone(t, carry):
        for d in range(1, ny):
            cy(t, d).wait_send()
            ycopy(0, t, d).wait_send()
            ycopy(1, t, d).wait_send()
        return carry

    lax.fori_loop(0, nr, ydone, 0)


def local(dims, tokens, gate_weight, up_weight, down_weight, out_grad):
    nx, ny, nz = dims
    nr = 2 * nx
    tb, dc = tokens.shape
    db, fb = gate_weight.shape
    t = nr * tb
    vm = pl.BlockSpec(memory_space=pltpu.VMEM)
    hbm = pl.BlockSpec(memory_space=pl.ANY)
    dma = pltpu.SemaphoreType.DMA
    half = nz // 2

    def sums(width):
        return [
            pltpu.VMEM((nx, tb, width), F32),
            pltpu.VMEM((nx, tb, width), F32),
            pltpu.VMEM((nx, tb, width), F32),
            pltpu.VMEM((nx, tb, width), BF),
            pltpu.VMEM((nx, tb, width), BF),
        ]

    def shares():
        return [
            pltpu.VMEM((nr, ny - 1, tb, dc), BF),
            pltpu.VMEM((nr, tb, dc), F32),
            pltpu.VMEM((nr, ny - 1, tb, dc), BF),
        ]

    scratch = [
        pltpu.VMEM((t, 2 * db), BF),
        pltpu.VMEM((db, 2 * fb), BF),
        pltpu.VMEM((fb, db), BF),
        pltpu.VMEM((t, fb), BF),
        pltpu.VMEM((t, 2 * fb), BF),
        pltpu.VMEM((ny, fb, dc), BF),
        pltpu.VMEM((ny, fb, dc), BF),
        *sums(2 * fb),
        *sums(fb),
        pltpu.VMEM((tb, db), F32),
        *shares(),
        *shares(),
        pltpu.VMEM((2, nz, tb, dc), BF),
        pltpu.VMEM((2, nz, tb, dc), BF),
        pltpu.VMEM((2, tb, dc), F32),
        pltpu.VMEM((2, tb, dc), BF),
        pltpu.VMEM((ny, fb, dc), BF),
        dma((2,)), dma((2,)), dma((ny,)), dma((ny,)),
        *[dma((2, half + 1))] * 4,
        dma((nr, ny - 1)), dma((nr, ny - 1)),
        *[dma((ny,))] * 8,
        *[dma((nx,))] * 16,
        *[dma((nr, ny - 1))] * 4,
        dma((2, nz)), dma((2, nz)), dma((2,)), dma((2,)), dma((3,)),
    ]
    shape = jax.ShapeDtypeStruct
    return pl.pallas_call(
        functools.partial(kernel, dims),
        out_shape=(
            shape((tb, dc), BF),
            shape((tb, dc), BF),
            shape((db, fb), BF),
            shape((db, fb), BF),
            shape((ny * fb, dc), BF),
        ),
        in_specs=[vm, vm, hbm, hbm, vm],
        out_specs=(vm,) * 5,
        scratch_shapes=scratch,
        compiler_params=pltpu.CompilerParams(
            collective_id=0, has_side_effects=True, vmem_limit_bytes=50 * 2**20
        ),
        name="swiglu",
    )(tokens, out_grad, gate_weight, up_weight, down_weight)


def solution(mesh):
    nr, nc = mesh.shape["row"], mesh.shape["col"]
    dims = (nr // 2, nc // nr, nr)
    spec = P("row", "col")
    return jax.shard_map(
        functools.partial(local, dims),
        mesh=mesh,
        in_specs=(spec,) * 5,
        out_specs=(spec,) * 5,
        check_vma=False,
    )
```

```python
import functools

import jax
import jax.numpy as jnp
from jax import lax
from jax.experimental import pallas as pl
from jax.experimental.pallas import tpu as pltpu
from jax.sharding import PartitionSpec as P

MESH = pl.DeviceIdType.MESH
BF = jnp.bfloat16
F32 = jnp.float32


def nn(a, b):
    return lax.dot_general(a, b, (((1,), (0,)), ((), ())), preferred_element_type=F32)


def nt(a, b):
    return lax.dot_general(a, b, (((1,), (1,)), ((), ())), preferred_element_type=F32)


def tn(a, b):
    return lax.dot_general(a, b, (((0,), (0,)), ((), ())), preferred_element_type=F32)


def kernel(
    dims,
    tok_hbm, cot_hbm, gate_hbm, up_hbm, down_hbm,
    out_o, tg_o, gg_o, ug_o, dg_o,
    tok, cot, down, xg, gw, dp, hh, hg, mid, mid2,
    acc_a, ms_a, mr_a, xs_a, xr_a,
    acc_b, ms_b, mr_b, xs_b, xr_b,
    o32, os_o, own_o, yr_o, os_t, own_t, yr_t,
    zs, zr, zown, fs, dgs,
    tos, tor, cos, cor, tys, tyr, cys, cyr,
    d1s, d1r, d2s, d2r, e1s, e1r, e2s, e2r,
    mas, mar, mbs, mbr, xas, xar, xbs, xbr,
    hxs, hxr, hms, hmr, gxs, gxr, gms, gmr,
    yos, yor, yts, ytr, zsm, zrm, f_s, f_r, lsem,
):
    nx, ny, nz = dims
    nr = 2 * nx
    tb, dc = tok.shape
    db, fb = gate_hbm.shape

    row, col = lax.axis_index("row"), lax.axis_index("col")
    x, kap = lax.div(row, 2), lax.rem(row, 2)
    z, y = lax.div(col, ny), lax.rem(col, ny)
    mate = (x * 2 + 1 - kap, col)
    diag = row == z
    twin = (z, row * ny + y)

    near = sorted({1, nx - 1})
    opposite = nx // 2 if nx > 2 else 0

    def xdev(d):
        return (lax.rem(x + d, nx) * 2 + kap, col)

    def ydev(d):
        return (row, z * ny + lax.rem(y + d, ny))

    def zdev(d):
        return (row, lax.rem(z + d, nz) * ny + y)

    def panel_to(d):
        return (z, lax.rem(z + d, nz) * ny + y)

    def panel_from(r):
        return (r, row * ny + y)

    def leg1_to(k):
        return (lax.rem(x + y - k + 1 + nx, nx) * 2 + kap, z * ny + k)

    def leg1_from(s):
        return (lax.rem(x + y - s - 1 + 2 * nx, nx) * 2 + kap, z * ny + s)

    def leg2_to(s):
        return (z, (lax.rem(x + y - s - 1 + 2 * nx, nx) * 2 + kap) * ny + y)

    def leg2_from(s):
        return (lax.rem(lax.div(z, 2) + s - y + 1 + nx, nx) * 2 + lax.rem(z, 2), row * ny + y)

    def leg2_home(s):
        return jnp.logical_and(diag, lax.rem(x + y - s - 1 + 2 * nx, nx) == x)

    def leg2_kept(s):
        return jnp.logical_and(diag, lax.rem(x + s - y + 1 + nx, nx) == x)

    def rows(t):
        return pl.ds(pl.multiple_of(t * tb, tb), tb)

    def lanes(k):
        return pl.ds(pl.multiple_of(k * dc, dc), dc)

    def frows(k):
        return pl.ds(pl.multiple_of(k * fb, fb), fb)

    def rc(src, dst, ss, rs, dev):
        return pltpu.make_async_remote_copy(
            src_ref=src, dst_ref=dst, send_sem=ss, recv_sem=rs,
            device_id=dev, device_id_type=MESH,
        )

    def hcopy(buf, t, ss, rs, dev):
        return rc(buf.at[rows(t)], buf.at[rows(t)], ss, rs, dev)

    def hhalf(buf, t, way, ss, rs, dev):
        ht = tb // 2
        ref = buf.at[pl.ds(pl.multiple_of(t * tb + way * ht, ht), ht)]
        return rc(ref, ref, ss, rs, dev)

    def no(cond):
        return jnp.logical_not(cond)

    loads = [
        pltpu.make_async_copy(src, dst, lsem.at[i])
        for i, (src, dst) in enumerate((
            (tok_hbm, tok),
            (cot_hbm, cot),
            (down_hbm, down),
            (gate_hbm, gw.at[:, pl.ds(0, fb)]),
            (up_hbm, gw.at[:, pl.ds(fb, fb)]),
        ))
    ]
    for load in loads:
        load.start()

    bar = pltpu.get_barrier_semaphore()

    def greet(dev):
        pl.semaphore_signal(bar, inc=1, device_id=dev, device_id_type=MESH)

    greet(mate)
    for d in range(1, nx):
        greet(xdev(d))
    for d in range(1, ny):
        greet(ydev(d))
    for d in range(1, nz):
        greet(zdev(d))

    count = 1 + (nx - 1) + (ny - 1) + (nz - 1) + 2 * ny
    for d in range(nz):
        @pl.when(no(jnp.logical_and(diag, d == 0)))
        def _():
            greet(panel_to(d))

        @pl.when(no(jnp.logical_and(diag, row == d)))
        def _():
            greet(panel_from(d))

        count = count + jnp.where(jnp.logical_and(diag, d == 0), 0, 1)
        count = count + jnp.where(jnp.logical_and(diag, row == d), 0, 1)
    for s in range(ny):
        greet(leg1_to(s))
        greet(leg1_from(s))

        @pl.when(no(leg2_home(s)))
        def _():
            greet(leg2_to(s))

        @pl.when(no(leg2_kept(s)))
        def _():
            greet(leg2_from(s))

        count = count + jnp.where(leg2_home(s), 0, 1) + jnp.where(leg2_kept(s), 0, 1)
    pl.semaphore_wait(bar, count)

    def sub(w, k):
        return lanes(w * ny + k)

    far_first = sorted(range(nz), key=lambda d: -min(d, nz - d))

    def panel_send(w):
        src, ss, sr = ((tok, tos, tor), (cot, cos, cor))[w]
        for d in far_first:
            @pl.when(no(jnp.logical_and(diag, d == 0)))
            def _():
                rc(src, xg.at[rows(row), sub(w, y)], ss.at[d], sr.at[row], panel_to(d)).start()

        @pl.when(diag)
        def _():
            xg[rows(row), sub(w, y)] = src[...]

    def panel_y(w, r, d):
        ss, sr = ((tys, tyr), (cys, cyr))[w]
        ref = xg.at[rows(r), sub(w, y)]
        return rc(ref, ref, ss.at[r, d - 1], sr.at[r, d - 1], ydev(d))

    def panel_pass(w, r):
        sr = (tor, cor)[w]

        @pl.when(no(jnp.logical_and(diag, row == r)))
        def _():
            ref = xg.at[rows(r), sub(w, y)]
            rc(ref, ref, sr.at[r], sr.at[r], panel_from(r)).wait_recv()

        for d in range(1, ny):
            panel_y(w, r, d).start()

    def panel_whole(w, r):
        sr = (tyr, cyr)[w]
        for d in range(1, ny):
            ref = xg.at[rows(r), sub(w, lax.rem(y - d + ny, ny))]
            rc(ref, ref, sr.at[r, d - 1], sr.at[r, d - 1], ydev(d)).wait_recv()

    def order(i):
        return lax.rem(x + 1 + lax.div(i, 2), nx) * 2 + lax.rem(i, 2)

    def leg2(src, dst_of, s1, r1, s2, r2, s):
        ref = src.at[s]
        rc(ref, ref, s1.at[s], r1.at[s], leg1_from(s)).wait_recv()

        @pl.when(no(leg2_home(s)))
        def _():
            rc(ref, dst_of(s), s2.at[s], r2.at[s], leg2_to(s)).start()

        @pl.when(leg2_home(s))
        def _():
            pltpu.make_async_copy(ref, dst_of(s), lsem.at[5]).start()
            pltpu.make_async_copy(ref, dst_of(s), lsem.at[5]).wait()

    def dp_at(s):
        return dp.at[:, lanes(s)]

    def dg_at(s):
        return dg_o.at[frows(s)]

    loads[2].wait()
    for k in range(ny):
        rc(down.at[frows(k)], mid.at[y], d1s.at[k], d1r.at[y], leg1_to(k)).start()

    loads[0].wait()
    panel_send(0)
    loads[1].wait()
    panel_send(1)

    for s in range(ny):
        leg2(mid, dp_at, d1s, d1r, d2s, d2r, s)

    def pass_tok(i, carry):
        panel_pass(0, order(i))
        return carry

    lax.fori_loop(0, nr, pass_tok, 0)
    loads[3].wait()
    loads[4].wait()

    def reduce_pair(t, acc, mr, xs, xr, ms_sem, mr_sem, xs_sem, xr_sem):
        xt = lax.div(t, 2)
        ref = mr.at[xt]
        rc(ref, ref, ms_sem.at[xt], mr_sem.at[xt], mate).wait_recv()

        @pl.when(xt == x)
        def _():
            acc[xt] = acc[xt] + mr[xt]

        @pl.when(xt != x)
        def _():
            d = lax.rem(xt - x + nx, nx)
            xs[d] = (acc[xt] + mr[xt]).astype(BF)
            rc(xs.at[d], xr.at[d], xs_sem.at[d], xr_sem.at[d], xdev(d)).start()

    set_a = (acc_a, mr_a, xs_a, xr_a, mas, mar, xas, xar)
    set_b = (acc_b, mr_b, xs_b, xr_b, mbs, mbr, xbs, xbr)

    def give(t, part, acc, ms, mr, s_sem, r_sem):
        xt = lax.div(t, 2)

        @pl.when(lax.rem(t, 2) == kap)
        def _():
            acc[xt] = part

        @pl.when(lax.rem(t, 2) != kap)
        def _():
            ms[xt] = part
            rc(ms.at[xt], mr.at[xt], s_sem.at[xt], r_sem.at[xt], mate).start()

    def step_a(i, carry):
        t = order(i)
        panel_whole(0, t)
        part = nn(xg[rows(t), pl.ds(0, db)], gw[...])
        give(t, part, acc_a, ms_a, mr_a, mas, mar)

        before = order(jnp.maximum(i - 1, 0))

        @pl.when(jnp.logical_and(i > 0, lax.rem(before, 2) == kap))
        def _():
            reduce_pair(before, *set_a)

        @pl.when(i >= nr // 2)
        def _():
            panel_pass(1, order(2 * i - nr))
            panel_pass(1, order(2 * i - nr + 1))

        return carry

    lax.fori_loop(0, nr, step_a, 0)

    @pl.when(lax.rem(order(nr - 1), 2) == kap)
    def _():
        reduce_pair(order(nr - 1), *set_a)

    chunk = 16

    def spot(i):
        r0 = pl.multiple_of(i * chunk, chunk)
        return pl.ds(r0, chunk), pl.ds(pl.multiple_of(row * tb + r0, chunk), chunk)

    for d in range(1, nx):
        rc(xr_a.at[d], xr_a.at[d], xas.at[d], xar.at[d], xdev(d)).wait_recv()

    def point_h(i, carry):
        here, there = spot(i)
        sa = acc_a[x, here, :]
        for d in range(1, nx):
            sa = sa + xr_a[d, here, :].astype(F32)
        acc_a[x, here, :] = sa
        g, u = sa[:, :fb], sa[:, fb:]
        hh[there, :] = (g * jax.nn.sigmoid(g) * u).astype(BF)
        return carry

    lax.fori_loop(0, tb // chunk, point_h, 0)

    def share(buf, xs_sem, xr_sem, ms_sem, mr_sem):
        for d in near:
            hcopy(buf, row, xs_sem.at[d], xr_sem.at[d], xdev(d)).start()
        hcopy(buf, row, ms_sem.at[0], mr_sem.at[0], mate).start()

    def kin(d):
        return lax.rem(x - d + nx, nx) * 2 + kap

    share(hh, hxs, hxr, hms, hmr)

    for s in range(ny):
        @pl.when(no(leg2_kept(s)))
        def _():
            rc(dp_at(s), dp_at(s), d2s.at[s], d2r.at[s], leg2_from(s)).wait_recv()

    def step_b(i, carry):
        t = order(i)
        panel_whole(1, t)
        part = nt(xg[rows(t), pl.ds(db, db)], dp[...])
        give(t, part, acc_b, ms_b, mr_b, mbs, mbr)

        before = order(jnp.maximum(i - 1, 0))

        @pl.when(jnp.logical_and(i > 0, lax.rem(before, 2) == kap))
        def _():
            reduce_pair(before, *set_b)

        return carry

    lax.fori_loop(0, nr, step_b, 0)

    @pl.when(lax.rem(order(nr - 1), 2) == kap)
    def _():
        reduce_pair(order(nr - 1), *set_b)

    def dist(j):
        q = lax.div(j, 2)
        return jnp.where(lax.rem(q, 2) == 1, lax.div(q + 1, 2), lax.rem(nx - lax.div(q, 2), nx))

    def block(j):
        src = lax.rem(x - dist(j) + nx, nx)
        return src * 2 + jnp.where(lax.rem(j, 2) == 0, kap, 1 - kap)

    def arrive(buf, j, xs_sem, xr_sem, ms_sem, mr_sem):
        t, d = block(j), dist(j)
        even = lax.rem(j, 2) == 0

        @pl.when(j == 2)
        def _():
            for e in near:
                hcopy(buf, kin(e), xs_sem.at[e], xr_sem.at[e], xdev(e)).wait_recv()
                if opposite:
                    way = 0 if e == 1 else 1
                    hhalf(buf, kin(e), way, xs_sem.at[2 + way * (nx - 2)], xr_sem.at[2 + way * (nx - 2)], xdev(e)).start()
            for e in near:
                hcopy(buf, kin(e), ms_sem.at[e], mr_sem.at[e], mate).start()

        if opposite:
            @pl.when(jnp.logical_and(even, d == opposite))
            def _():
                for way in range(2):
                    sem = xr_sem.at[2 + way * (nx - 2)]
                    hhalf(buf, t, way, sem, sem, xdev(1)).wait_recv()
                hcopy(buf, t, ms_sem.at[d], mr_sem.at[d], mate).start()

        @pl.when(no(even))
        def _():
            hcopy(buf, t, ms_sem.at[d], mr_sem.at[d], mate).wait_recv()

    def ycopy(w, t, d):
        os, yr, ss, rs = ((os_o, yr_o, yos, yor), (os_t, yr_t, yts, ytr))[w]
        return rc(os.at[t, d - 1], yr.at[t, d - 1], ss.at[t, d - 1], rs.at[t, d - 1], ydev(d))

    def spread(w, t, part):
        os, own = ((os_o, own_o), (os_t, own_t))[w]
        o32[...] = part
        for e in range(1, ny):
            os[t, e - 1] = o32[:, lanes(lax.rem(y + e, ny))].astype(BF)
            ycopy(w, t, e).start()
        own[t] = o32[:, lanes(y)]

    def zcopy(w, d):
        return rc(zs.at[w, d], zr.at[w, d], zsm.at[w, d], zrm.at[w, d], zdev(d))

    def reduce_y(w, t):
        own, yr = ((own_o, yr_o), (own_t, yr_t))[w]
        total = own[t]
        for d in range(1, ny):
            ycopy(w, t, d).wait_recv()
            total = total + yr[t, d - 1].astype(F32)

        @pl.when(t == z)
        def _():
            zown[w] = total

        @pl.when(t != z)
        def _():
            d = lax.rem(t - z + nz, nz)
            zs[w, d] = total.astype(BF)
            zcopy(w, d).start()

    def step_c(j, carry):
        arrive(hh, j, hxs, hxr, hms, hmr)
        t = block(j)
        spread(0, t, nn(hh[rows(t), :], dp[...]))
        return carry

    lax.fori_loop(0, nr, step_c, 0)

    for k in range(ny):
        dgs[k] = tn(hh[...], xg[:, pl.ds(db + k * dc, dc)]).astype(BF)
        rc(dgs.at[k], mid2.at[y], e1s.at[k], e1r.at[y], leg1_to(k)).start()

    for d in range(1, nx):
        rc(xr_b.at[d], xr_b.at[d], xbs.at[d], xbr.at[d], xdev(d)).wait_recv()

    def point_g(i, carry):
        here, there = spot(i)
        sa = acc_a[x, here, :]
        sb = acc_b[x, here, :]
        for d in range(1, nx):
            sb = sb + xr_b[d, here, :].astype(F32)
        g, u = sa[:, :fb], sa[:, fb:]
        sig = jax.nn.sigmoid(g)
        hg[there, pl.ds(0, fb)] = (sb * u * sig * (1.0 + g * (1.0 - sig))).astype(BF)
        hg[there, pl.ds(fb, fb)] = (sb * (g * sig)).astype(BF)
        return carry

    lax.fori_loop(0, tb // chunk, point_g, 0)
    share(hg, gxs, gxr, gms, gmr)

    for s in range(ny):
        leg2(mid2, dg_at, e1s, e1r, e2s, e2r, s)

    lag = 2

    def step_d(j, carry):
        arrive(hg, j, gxs, gxr, gms, gmr)
        t = block(j)
        spread(1, t, nt(hg[rows(t), :], gw[...]))
        reduce_y(0, t)

        @pl.when(j >= lag)
        def _():
            reduce_y(1, block(jnp.maximum(j - lag, 0)))

        return carry

    lax.fori_loop(0, nr, step_d, 0)

    for k in range(ny):
        w = tn(xg[:, pl.ds(k * dc, dc)], hg[...]).astype(BF)
        gg_o[pl.ds(k * dc, dc)] = w[:, :fb]
        ug_o[pl.ds(k * dc, dc)] = w[:, fb:]

    for j in range(nr - lag, nr):
        reduce_y(1, block(j))

    def fcopy(w):
        return rc(fs.at[w], (out_o, tg_o)[w], f_s.at[w], f_r.at[w], twin)

    for w in range(2):
        total = zown[w]
        for d in range(1, nz):
            zcopy(w, d).wait_recv()
            total = total + zr[w, d].astype(F32)
        fs[w] = total.astype(BF)

        @pl.when(diag)
        def _():
            (out_o, tg_o)[w][...] = fs[w]

        @pl.when(no(diag))
        def _():
            fcopy(w).start()

    @pl.when(no(diag))
    def _():
        for w in range(2):
            fcopy(w).wait_recv()

    for s in range(ny):
        @pl.when(no(leg2_kept(s)))
        def _():
            rc(dg_at(s), dg_at(s), e2s.at[s], e2r.at[s], leg2_from(s)).wait_recv()

    @pl.when(no(diag))
    def _():
        for w in range(2):
            fcopy(w).wait_send()

    for k in range(ny):
        rc(dgs.at[k], mid.at[k], d1s.at[k], d1r.at[k], leg1_to(k)).wait_send()
        rc(dgs.at[k], mid.at[k], e1s.at[k], e1r.at[k], leg1_to(k)).wait_send()

        @pl.when(no(leg2_home(k)))
        def _():
            rc(mid.at[k], dp_at(k), d2s.at[k], d2r.at[k], leg2_to(k)).wait_send()
            rc(mid2.at[k], dg_at(k), e2s.at[k], e2r.at[k], leg2_to(k)).wait_send()

    for d in range(nz):
        @pl.when(no(jnp.logical_and(diag, d == 0)))
        def _():
            rc(tok, tok, tos.at[d], tor.at[d], panel_to(d)).wait_send()
            rc(cot, cot, cos.at[d], cor.at[d], panel_to(d)).wait_send()

    for q in range(nx):
        rc(ms_a.at[q], mr_a.at[q], mas.at[q], mar.at[q], mate).wait_send()
        rc(ms_b.at[q], mr_b.at[q], mbs.at[q], mbr.at[q], mate).wait_send()
        hcopy(hh, row, hms.at[q], hmr.at[q], mate).wait_send()
        hcopy(hg, row, gms.at[q], gmr.at[q], mate).wait_send()
    for d in range(1, nx):
        rc(xs_a.at[d], xr_a.at[d], xas.at[d], xar.at[d], xdev(d)).wait_send()
        rc(xs_b.at[d], xr_b.at[d], xbs.at[d], xbr.at[d], xdev(d)).wait_send()
    for d in near:
        hcopy(hh, row, hxs.at[d], hxr.at[d], xdev(d)).wait_send()
        hcopy(hg, row, gxs.at[d], gxr.at[d], xdev(d)).wait_send()
    if opposite:
        for e in (2, nx):
            hhalf(hh, row, 0, hxs.at[e], hxr.at[e], xdev(1)).wait_send()
            hhalf(hg, row, 0, gxs.at[e], gxr.at[e], xdev(1)).wait_send()
    for d in range(1, nz):
        zcopy(0, d).wait_send()
        zcopy(1, d).wait_send()

    def ydone(t, carry):
        for d in range(1, ny):
            panel_y(0, t, d).wait_send()
            panel_y(1, t, d).wait_send()
            ycopy(0, t, d).wait_send()
            ycopy(1, t, d).wait_send()
        return carry

    lax.fori_loop(0, nr, ydone, 0)


def local(dims, tokens, gate_weight, up_weight, down_weight, out_grad):
    nx, ny, nz = dims
    nr = 2 * nx
    tb, dc = tokens.shape
    db, fb = gate_weight.shape
    t = nr * tb
    vm = pl.BlockSpec(memory_space=pltpu.VMEM)
    hbm = pl.BlockSpec(memory_space=pl.ANY)
    dma = pltpu.SemaphoreType.DMA

    def sums(width):
        return [
            pltpu.VMEM((nx, tb, width), F32),
            pltpu.VMEM((nx, tb, width), F32),
            pltpu.VMEM((nx, tb, width), F32),
            pltpu.VMEM((nx, tb, width), BF),
            pltpu.VMEM((nx, tb, width), BF),
        ]

    def shares():
        return [
            pltpu.VMEM((nr, ny - 1, tb, dc), BF),
            pltpu.VMEM((nr, tb, dc), F32),
            pltpu.VMEM((nr, ny - 1, tb, dc), BF),
        ]

    scratch = [
        pltpu.VMEM((tb, dc), BF),
        pltpu.VMEM((tb, dc), BF),
        pltpu.VMEM((ny * fb, dc), BF),
        pltpu.VMEM((t, 2 * db), BF),
        pltpu.VMEM((db, 2 * fb), BF),
        pltpu.VMEM((fb, db), BF),
        pltpu.VMEM((t, fb), BF),
        pltpu.VMEM((t, 2 * fb), BF),
        pltpu.VMEM((ny, fb, dc), BF),
        pltpu.VMEM((ny, fb, dc), BF),
        *sums(2 * fb),
        *sums(fb),
        pltpu.VMEM((tb, db), F32),
        *shares(),
        *shares(),
        pltpu.VMEM((2, nz, tb, dc), BF),
        pltpu.VMEM((2, nz, tb, dc), BF),
        pltpu.VMEM((2, tb, dc), F32),
        pltpu.VMEM((2, tb, dc), BF),
        pltpu.VMEM((ny, fb, dc), BF),
        dma((nz,)), dma((nr,)), dma((nz,)), dma((nr,)),
        *[dma((nr, ny - 1))] * 4,
        *[dma((ny,))] * 8,
        *[dma((nx,))] * 8,
        *[dma((nx + 1,))] * 8,
        *[dma((nr, ny - 1))] * 4,
        dma((2, nz)), dma((2, nz)), dma((2,)), dma((2,)), dma((6,)),
    ]
    shape = jax.ShapeDtypeStruct
    return pl.pallas_call(
        functools.partial(kernel, dims),
        out_shape=(
            shape((tb, dc), BF),
            shape((tb, dc), BF),
            shape((db, fb), BF),
            shape((db, fb), BF),
            shape((ny * fb, dc), BF),
        ),
        in_specs=[hbm] * 5,
        out_specs=(vm,) * 5,
        scratch_shapes=scratch,
        compiler_params=pltpu.CompilerParams(
            collective_id=0, has_side_effects=True, vmem_limit_bytes=60 * 2**20
        ),
        name="swiglu",
    )(tokens, out_grad, gate_weight, up_weight, down_weight)


def solution(mesh):
    nr, nc = mesh.shape["row"], mesh.shape["col"]
    dims = (nr // 2, nc // nr, nr)
    spec = P("row", "col")
    return jax.shard_map(
        functools.partial(local, dims),
        mesh=mesh,
        in_specs=(spec,) * 5,
        out_specs=(spec,) * 5,
        check_vma=False,
    )
```

```python
import functools

import jax
import jax.numpy as jnp
from jax import lax
from jax.experimental import pallas as pl
from jax.experimental.pallas import tpu as pltpu
from jax.sharding import PartitionSpec as P

MESH = pl.DeviceIdType.MESH
BF = jnp.bfloat16
F32 = jnp.float32


def nn(a, b):
    return lax.dot_general(a, b, (((1,), (0,)), ((), ())), preferred_element_type=F32)


def nt(a, b):
    return lax.dot_general(a, b, (((1,), (1,)), ((), ())), preferred_element_type=F32)


def tn(a, b):
    return lax.dot_general(a, b, (((0,), (0,)), ((), ())), preferred_element_type=F32)


def kernel(
    dims,
    tok_hbm, cot_hbm, gate_hbm, up_hbm, down_hbm,
    out_o, tg_o, gg_o, ug_o, dg_o,
    tok, cot, down, xg, gw, dp, hh, hg, mid, mid2,
    acc_a, ms_a, mr_a, xs_a, xr_a,
    acc_b, ms_b, mr_b, xs_b, xr_b,
    o32, os_o, own_o, yr_o, os_t, own_t, yr_t,
    zs, zr, zown, fs, dgs, wgs,
    tos, tor, cos, cor, tys, tyr, cys, cyr,
    d1s, d1r, d2s, d2r, e1s, e1r, e2s, e2r,
    mas, mar, mbs, mbr, xas, xar, xbs, xbr,
    hxs, hxr, hms, hmr, gxs, gxr, gms, gmr,
    yos, yor, yts, ytr, zsm, zrm, f_s, f_r, lsem,
):
    nx, ny, nz = dims
    nr = 2 * nx
    tb, dc = tok.shape
    db, fb = gate_hbm.shape

    row, col = lax.axis_index("row"), lax.axis_index("col")
    x, kap = lax.div(row, 2), lax.rem(row, 2)
    z, y = lax.div(col, ny), lax.rem(col, ny)
    mate = (x * 2 + 1 - kap, col)
    diag = row == z
    twin = (z, row * ny + y)

    near = sorted({1, nx - 1})
    opposite = nx // 2 if nx > 2 else 0

    near_y = sorted({1, ny - 1})
    far_y = ny // 2 if ny > 2 else 0

    def xdev(d):
        return (lax.rem(x + d, nx) * 2 + kap, col)

    def ydev(d):
        return (row, z * ny + lax.rem(y + d, ny))

    def zdev(d):
        return (row, lax.rem(z + d, nz) * ny + y)

    def panel_to(d):
        return (z, lax.rem(z + d, nz) * ny + y)

    def panel_from(r):
        return (r, row * ny + y)

    def leg1_to(k):
        return (lax.rem(x + y - k + 1 + nx, nx) * 2 + kap, z * ny + k)

    def leg1_from(s):
        return (lax.rem(x + y - s - 1 + 2 * nx, nx) * 2 + kap, z * ny + s)

    def leg2_to(s):
        return (z, (lax.rem(x + y - s - 1 + 2 * nx, nx) * 2 + kap) * ny + y)

    def leg2_from(s):
        return (lax.rem(lax.div(z, 2) + s - y + 1 + nx, nx) * 2 + lax.rem(z, 2), row * ny + y)

    def leg2_home(s):
        return jnp.logical_and(diag, lax.rem(x + y - s - 1 + 2 * nx, nx) == x)

    def leg2_kept(s):
        return jnp.logical_and(diag, lax.rem(x + s - y + 1 + nx, nx) == x)

    def rows(t):
        return pl.ds(pl.multiple_of(t * tb, tb), tb)

    def lanes(k):
        return pl.ds(pl.multiple_of(k * dc, dc), dc)

    def frows(k):
        return pl.ds(pl.multiple_of(k * fb, fb), fb)

    def rc(src, dst, ss, rs, dev):
        return pltpu.make_async_remote_copy(
            src_ref=src, dst_ref=dst, send_sem=ss, recv_sem=rs,
            device_id=dev, device_id_type=MESH,
        )

    def hcopy(buf, t, ss, rs, dev):
        return rc(buf.at[rows(t)], buf.at[rows(t)], ss, rs, dev)

    def hhalf(buf, t, way, ss, rs, dev):
        ht = tb // 2
        ref = buf.at[pl.ds(pl.multiple_of(t * tb + way * ht, ht), ht)]
        return rc(ref, ref, ss, rs, dev)

    def no(cond):
        return jnp.logical_not(cond)

    loads = [
        pltpu.make_async_copy(src, dst, lsem.at[i])
        for i, (src, dst) in enumerate((
            (tok_hbm, tok),
            (cot_hbm, cot),
            (down_hbm, down),
            (gate_hbm, gw.at[:, pl.ds(0, fb)]),
            (up_hbm, gw.at[:, pl.ds(fb, fb)]),
        ))
    ]
    for load in loads:
        load.start()

    bar = pltpu.get_barrier_semaphore()

    def greet(dev):
        pl.semaphore_signal(bar, inc=1, device_id=dev, device_id_type=MESH)

    greet(mate)
    for d in range(1, nx):
        greet(xdev(d))
    for d in range(1, ny):
        greet(ydev(d))
    for d in range(1, nz):
        greet(zdev(d))

    count = 1 + (nx - 1) + (ny - 1) + (nz - 1) + 2 * ny
    for d in range(nz):
        @pl.when(no(jnp.logical_and(diag, d == 0)))
        def _():
            greet(panel_to(d))

        @pl.when(no(jnp.logical_and(diag, row == d)))
        def _():
            greet(panel_from(d))

        count = count + jnp.where(jnp.logical_and(diag, d == 0), 0, 1)
        count = count + jnp.where(jnp.logical_and(diag, row == d), 0, 1)
    for s in range(ny):
        greet(leg1_to(s))
        greet(leg1_from(s))

        @pl.when(no(leg2_home(s)))
        def _():
            greet(leg2_to(s))

        @pl.when(no(leg2_kept(s)))
        def _():
            greet(leg2_from(s))

        count = count + jnp.where(leg2_home(s), 0, 1) + jnp.where(leg2_kept(s), 0, 1)
    pl.semaphore_wait(bar, count)

    def sub(w, k):
        return lanes(w * ny + k)

    far_first = sorted(range(nz), key=lambda d: -min(d, nz - d))

    def panel_send(w):
        src, ss, sr = ((tok, tos, tor), (cot, cos, cor))[w]
        for d in far_first:
            @pl.when(no(jnp.logical_and(diag, d == 0)))
            def _():
                rc(src, xg.at[rows(row), sub(w, y)], ss.at[d], sr.at[row], panel_to(d)).start()

        @pl.when(diag)
        def _():
            xg[rows(row), sub(w, y)] = src[...]

    def panel_y(w, r, d):
        ss, sr = ((tys, tyr), (cys, cyr))[w]
        ref = xg.at[rows(r), sub(w, y)]
        return rc(ref, ref, ss.at[r, d - 1], sr.at[r, d - 1], ydev(d))

    def panel_pass(w, r):
        sr = (tor, cor)[w]

        @pl.when(no(jnp.logical_and(diag, row == r)))
        def _():
            ref = xg.at[rows(r), sub(w, y)]
            rc(ref, ref, sr.at[r], sr.at[r], panel_from(r)).wait_recv()

        for d in near_y:
            panel_y(w, r, d).start()

    def panel_from_y(w, r, d, dev):
        ss, sr = ((tys, tyr), (cys, cyr))[w]
        ref = xg.at[rows(r), sub(w, lax.rem(y - d + ny, ny))]
        return rc(ref, ref, ss.at[r, d - 1], sr.at[r, d - 1], dev)

    def panel_next(w, r):
        for d in near_y:
            panel_from_y(w, r, d, ydev(d)).wait_recv()
        if far_y:
            sr = (tyr, cyr)[w]
            ss = (tys, cys)[w]
            for side, d in enumerate(near_y):
                @pl.when(lax.rem(r, 2) == side)
                def _():
                    ref = xg.at[rows(r), sub(w, lax.rem(y - d + ny, ny))]
                    rc(ref, ref, ss.at[r, far_y - 1], sr.at[r, far_y - 1], ydev(d)).start()

    def panel_whole(w, r):
        if far_y:
            panel_from_y(w, r, far_y, ydev(1)).wait_recv()

    def order(i):
        return lax.rem(x + 1 + lax.div(i, 2), nx) * 2 + lax.rem(i, 2)

    def leg2(src, dst_of, s1, r1, s2, r2, s):
        ref = src.at[s]
        rc(ref, ref, s1.at[s], r1.at[s], leg1_from(s)).wait_recv()

        @pl.when(no(leg2_home(s)))
        def _():
            rc(ref, dst_of(s), s2.at[s], r2.at[s], leg2_to(s)).start()

        @pl.when(leg2_home(s))
        def _():
            pltpu.make_async_copy(ref, dst_of(s), lsem.at[5]).start()
            pltpu.make_async_copy(ref, dst_of(s), lsem.at[5]).wait()

    def dp_at(s):
        return dp.at[:, lanes(s)]

    def dg_at(s):
        return dg_o.at[frows(s)]

    loads[0].wait()
    panel_send(0)
    loads[2].wait()
    for k in range(ny):
        rc(down.at[frows(k)], mid.at[y], d1s.at[k], d1r.at[y], leg1_to(k)).start()

    loads[1].wait()
    panel_send(1)

    def pass_tok(i, carry):
        panel_pass(0, order(i))
        return carry

    lax.fori_loop(0, nr, pass_tok, 0)
    loads[3].wait()
    loads[4].wait()

    def reduce_pair(t, acc, mr, xs, xr, ms_sem, mr_sem, xs_sem, xr_sem):
        xt = lax.div(t, 2)
        ref = mr.at[xt]
        rc(ref, ref, ms_sem.at[xt], mr_sem.at[xt], mate).wait_recv()

        @pl.when(xt == x)
        def _():
            acc[xt] = acc[xt] + mr[xt]

        @pl.when(xt != x)
        def _():
            d = lax.rem(xt - x + nx, nx)
            xs[d] = (acc[xt] + mr[xt]).astype(BF)
            rc(xs.at[d], xr.at[d], xs_sem.at[d], xr_sem.at[d], xdev(d)).start()

    set_a = (acc_a, mr_a, xs_a, xr_a, mas, mar, xas, xar)
    set_b = (acc_b, mr_b, xs_b, xr_b, mbs, mbr, xbs, xbr)

    def give(t, part, acc, ms, mr, s_sem, r_sem):
        xt = lax.div(t, 2)

        @pl.when(lax.rem(t, 2) == kap)
        def _():
            acc[xt] = part

        @pl.when(lax.rem(t, 2) != kap)
        def _():
            ms[xt] = part
            rc(ms.at[xt], mr.at[xt], s_sem.at[xt], r_sem.at[xt], mate).start()

    for s in range(ny):
        leg2(mid, dp_at, d1s, d1r, d2s, d2r, s)

    ahead = 2
    for i in range(ahead):
        panel_next(0, order(i))

    def step_a(i, carry):
        t = order(i)

        @pl.when(i + ahead < nr)
        def _():
            panel_next(0, order(i + ahead))

        panel_whole(0, t)
        part = nn(xg[rows(t), pl.ds(0, db)], gw[...])
        give(t, part, acc_a, ms_a, mr_a, mas, mar)

        before = order(jnp.maximum(i - 1, 0))

        @pl.when(jnp.logical_and(i > 0, lax.rem(before, 2) == kap))
        def _():
            reduce_pair(before, *set_a)

        @pl.when(i >= nr // 2)
        def _():
            panel_pass(1, order(2 * i - nr))
            panel_pass(1, order(2 * i - nr + 1))

        return carry

    lax.fori_loop(0, nr, step_a, 0)

    @pl.when(lax.rem(order(nr - 1), 2) == kap)
    def _():
        reduce_pair(order(nr - 1), *set_a)

    def next_cot(i, carry):
        panel_next(1, order(i))
        return carry

    lax.fori_loop(0, nr, next_cot, 0)

    chunk = 16

    def spot(i):
        r0 = pl.multiple_of(i * chunk, chunk)
        return pl.ds(r0, chunk), pl.ds(pl.multiple_of(row * tb + r0, chunk), chunk)

    for d in range(1, nx):
        rc(xr_a.at[d], xr_a.at[d], xas.at[d], xar.at[d], xdev(d)).wait_recv()

    def point_h(i, carry):
        here, there = spot(i)
        sa = acc_a[x, here, :]
        for d in range(1, nx):
            sa = sa + xr_a[d, here, :].astype(F32)
        acc_a[x, here, :] = sa
        g, u = sa[:, :fb], sa[:, fb:]
        hh[there, :] = (g * jax.nn.sigmoid(g) * u).astype(BF)
        return carry

    lax.fori_loop(0, tb // chunk, point_h, 0)

    def share(buf, xs_sem, xr_sem, ms_sem, mr_sem):
        for d in near:
            hcopy(buf, row, xs_sem.at[d], xr_sem.at[d], xdev(d)).start()
        hcopy(buf, row, ms_sem.at[0], mr_sem.at[0], mate).start()

    def kin(d):
        return lax.rem(x - d + nx, nx) * 2 + kap

    share(hh, hxs, hxr, hms, hmr)

    for s in range(ny):
        @pl.when(no(leg2_kept(s)))
        def _():
            rc(dp_at(s), dp_at(s), d2s.at[s], d2r.at[s], leg2_from(s)).wait_recv()

    def step_b(i, carry):
        t = order(i)
        panel_whole(1, t)
        part = nt(xg[rows(t), pl.ds(db, db)], dp[...])
        give(t, part, acc_b, ms_b, mr_b, mbs, mbr)

        before = order(jnp.maximum(i - 1, 0))

        @pl.when(jnp.logical_and(i > 0, lax.rem(before, 2) == kap))
        def _():
            reduce_pair(before, *set_b)

        return carry

    lax.fori_loop(0, nr, step_b, 0)

    @pl.when(lax.rem(order(nr - 1), 2) == kap)
    def _():
        reduce_pair(order(nr - 1), *set_b)

    def dist(j):
        q = lax.div(j, 2)
        return jnp.where(lax.rem(q, 2) == 1, lax.div(q + 1, 2), lax.rem(nx - lax.div(q, 2), nx))

    def block(j):
        src = lax.rem(x - dist(j) + nx, nx)
        return src * 2 + jnp.where(lax.rem(j, 2) == 0, kap, 1 - kap)

    def arrive(buf, j, xs_sem, xr_sem, ms_sem, mr_sem):
        t, d = block(j), dist(j)
        even = lax.rem(j, 2) == 0

        @pl.when(j == 2)
        def _():
            for e in near:
                hcopy(buf, kin(e), xs_sem.at[e], xr_sem.at[e], xdev(e)).wait_recv()
                if opposite:
                    way = 0 if e == 1 else 1
                    hhalf(buf, kin(e), way, xs_sem.at[2 + way * (nx - 2)], xr_sem.at[2 + way * (nx - 2)], xdev(e)).start()
            for e in near:
                hcopy(buf, kin(e), ms_sem.at[e], mr_sem.at[e], mate).start()

        if opposite:
            @pl.when(jnp.logical_and(even, d == opposite))
            def _():
                for way in range(2):
                    sem = xr_sem.at[2 + way * (nx - 2)]
                    hhalf(buf, t, way, sem, sem, xdev(1)).wait_recv()
                hcopy(buf, t, ms_sem.at[d], mr_sem.at[d], mate).start()

        @pl.when(no(even))
        def _():
            hcopy(buf, t, ms_sem.at[d], mr_sem.at[d], mate).wait_recv()

    def ycopy(w, t, d):
        os, yr, ss, rs = ((os_o, yr_o, yos, yor), (os_t, yr_t, yts, ytr))[w]
        return rc(os.at[t, d - 1], yr.at[t, d - 1], ss.at[t, d - 1], rs.at[t, d - 1], ydev(d))

    def spread(w, t, part):
        os, own = ((os_o, own_o), (os_t, own_t))[w]
        o32[...] = part
        for e in range(1, ny):
            os[t, e - 1] = o32[:, lanes(lax.rem(y + e, ny))].astype(BF)
            ycopy(w, t, e).start()
        own[t] = o32[:, lanes(y)]

    def zcopy(w, d):
        return rc(zs.at[w, d], zr.at[w, d], zsm.at[w, d], zrm.at[w, d], zdev(d))

    def reduce_y(w, t):
        own, yr = ((own_o, yr_o), (own_t, yr_t))[w]
        total = own[t]
        for d in range(1, ny):
            ycopy(w, t, d).wait_recv()
            total = total + yr[t, d - 1].astype(F32)

        @pl.when(t == z)
        def _():
            zown[w] = total

        @pl.when(t != z)
        def _():
            d = lax.rem(t - z + nz, nz)
            zs[w, d] = total.astype(BF)
            zcopy(w, d).start()

    def step_c(j, carry):
        arrive(hh, j, hxs, hxr, hms, hmr)
        t = block(j)
        spread(0, t, nn(hh[rows(t), :], dp[...]))
        return carry

    lax.fori_loop(0, nr, step_c, 0)

    for k in range(ny):
        dgs[k] = tn(hh[...], xg[:, pl.ds(db + k * dc, dc)]).astype(BF)
        rc(dgs.at[k], mid2.at[y], e1s.at[k], e1r.at[y], leg1_to(k)).start()

    for d in range(1, nx):
        rc(xr_b.at[d], xr_b.at[d], xbs.at[d], xbr.at[d], xdev(d)).wait_recv()

    def point_g(i, carry):
        here, there = spot(i)
        sa = acc_a[x, here, :]
        sb = acc_b[x, here, :]
        for d in range(1, nx):
            sb = sb + xr_b[d, here, :].astype(F32)
        g, u = sa[:, :fb], sa[:, fb:]
        sig = jax.nn.sigmoid(g)
        hg[there, pl.ds(0, fb)] = (sb * u * sig * (1.0 + g * (1.0 - sig))).astype(BF)
        hg[there, pl.ds(fb, fb)] = (sb * (g * sig)).astype(BF)
        return carry

    lax.fori_loop(0, tb // chunk, point_g, 0)
    share(hg, gxs, gxr, gms, gmr)

    for s in range(ny):
        leg2(mid2, dg_at, e1s, e1r, e2s, e2r, s)

    lag = 2

    def step_d(j, carry):
        arrive(hg, j, gxs, gxr, gms, gmr)
        t = block(j)
        spread(1, t, nt(hg[rows(t), :], gw[...]))
        reduce_y(0, t)

        @pl.when(j >= lag)
        def _():
            reduce_y(1, block(jnp.maximum(j - lag, 0)))

        return carry

    lax.fori_loop(0, nr, step_d, 0)

    for j in range(nr - lag, nr):
        reduce_y(1, block(j))

    for k in range(ny):
        w = tn(xg[:, pl.ds(k * dc, dc)], hg[...]).astype(BF)
        wgs[pl.ds(k * dc, dc)] = w

    grads = [
        pltpu.make_async_copy(wgs.at[:, pl.ds(i * fb, fb)], dst, lsem.at[i])
        for i, dst in enumerate((gg_o, ug_o))
    ]
    for copy in grads:
        copy.start()

    def fcopy(w):
        return rc(fs.at[w], (out_o, tg_o)[w], f_s.at[w], f_r.at[w], twin)

    for w in range(2):
        total = zown[w]
        for d in range(1, nz):
            zcopy(w, d).wait_recv()
            total = total + zr[w, d].astype(F32)
        fs[w] = total.astype(BF)

        @pl.when(diag)
        def _():
            kept = pltpu.make_async_copy(fs.at[w], (out_o, tg_o)[w], lsem.at[5])
            kept.start()
            kept.wait()

        @pl.when(no(diag))
        def _():
            fcopy(w).start()

    @pl.when(no(diag))
    def _():
        for w in range(2):
            fcopy(w).wait_recv()

    for s in range(ny):
        @pl.when(no(leg2_kept(s)))
        def _():
            rc(dg_at(s), dg_at(s), e2s.at[s], e2r.at[s], leg2_from(s)).wait_recv()

    for copy in grads:
        copy.wait()

    @pl.when(no(diag))
    def _():
        for w in range(2):
            fcopy(w).wait_send()

    for k in range(ny):
        rc(dgs.at[k], mid.at[k], d1s.at[k], d1r.at[k], leg1_to(k)).wait_send()
        rc(dgs.at[k], mid.at[k], e1s.at[k], e1r.at[k], leg1_to(k)).wait_send()

        @pl.when(no(leg2_home(k)))
        def _():
            rc(mid.at[k], dp_at(k), d2s.at[k], d2r.at[k], leg2_to(k)).wait_send()
            rc(mid2.at[k], dg_at(k), e2s.at[k], e2r.at[k], leg2_to(k)).wait_send()

    for d in range(nz):
        @pl.when(no(jnp.logical_and(diag, d == 0)))
        def _():
            rc(tok, tok, tos.at[d], tor.at[d], panel_to(d)).wait_send()
            rc(cot, cot, cos.at[d], cor.at[d], panel_to(d)).wait_send()

    for q in range(nx):
        rc(ms_a.at[q], mr_a.at[q], mas.at[q], mar.at[q], mate).wait_send()
        rc(ms_b.at[q], mr_b.at[q], mbs.at[q], mbr.at[q], mate).wait_send()
        hcopy(hh, row, hms.at[q], hmr.at[q], mate).wait_send()
        hcopy(hg, row, gms.at[q], gmr.at[q], mate).wait_send()
    for d in range(1, nx):
        rc(xs_a.at[d], xr_a.at[d], xas.at[d], xar.at[d], xdev(d)).wait_send()
        rc(xs_b.at[d], xr_b.at[d], xbs.at[d], xbr.at[d], xdev(d)).wait_send()
    for d in near:
        hcopy(hh, row, hxs.at[d], hxr.at[d], xdev(d)).wait_send()
        hcopy(hg, row, gxs.at[d], gxr.at[d], xdev(d)).wait_send()
    if opposite:
        for e in (2, nx):
            hhalf(hh, row, 0, hxs.at[e], hxr.at[e], xdev(1)).wait_send()
            hhalf(hg, row, 0, gxs.at[e], gxr.at[e], xdev(1)).wait_send()
    for d in range(1, nz):
        zcopy(0, d).wait_send()
        zcopy(1, d).wait_send()

    def ydone(t, carry):
        for d in range(1, ny):
            panel_y(0, t, d).wait_send()
            panel_y(1, t, d).wait_send()
            ycopy(0, t, d).wait_send()
            ycopy(1, t, d).wait_send()
        return carry

    lax.fori_loop(0, nr, ydone, 0)


def place(*refs):
    sems = refs[-1]
    copies = [
        pltpu.make_async_copy(src, dst, sems.at[i])
        for i, (src, dst) in enumerate(zip(refs[:5], refs[5:10]))
    ]
    for copy in copies:
        copy.start()
    for copy in copies:
        copy.wait()


def local(dims, tokens, gate_weight, up_weight, down_weight, out_grad):
    nx, ny, nz = dims
    nr = 2 * nx
    tb, dc = tokens.shape
    db, fb = gate_weight.shape
    t = nr * tb
    hbm = pl.BlockSpec(memory_space=pl.ANY)
    dma = pltpu.SemaphoreType.DMA

    def sums(width):
        return [
            pltpu.VMEM((nx, tb, width), F32),
            pltpu.VMEM((nx, tb, width), F32),
            pltpu.VMEM((nx, tb, width), F32),
            pltpu.VMEM((nx, tb, width), BF),
            pltpu.VMEM((nx, tb, width), BF),
        ]

    def shares():
        return [
            pltpu.VMEM((nr, ny - 1, tb, dc), BF),
            pltpu.VMEM((nr, tb, dc), F32),
            pltpu.VMEM((nr, ny - 1, tb, dc), BF),
        ]

    scratch = [
        pltpu.VMEM((tb, dc), BF),
        pltpu.VMEM((tb, dc), BF),
        pltpu.VMEM((ny * fb, dc), BF),
        pltpu.VMEM((t, 2 * db), BF),
        pltpu.VMEM((db, 2 * fb), BF),
        pltpu.VMEM((fb, db), BF),
        pltpu.VMEM((t, fb), BF),
        pltpu.VMEM((t, 2 * fb), BF),
        pltpu.VMEM((ny, fb, dc), BF),
        pltpu.VMEM((ny, fb, dc), BF),
        *sums(2 * fb),
        *sums(fb),
        pltpu.VMEM((tb, db), F32),
        *shares(),
        *shares(),
        pltpu.VMEM((2, nz, tb, dc), BF),
        pltpu.VMEM((2, nz, tb, dc), BF),
        pltpu.VMEM((2, tb, dc), F32),
        pltpu.VMEM((2, tb, dc), BF),
        pltpu.VMEM((ny, fb, dc), BF),
        pltpu.VMEM((db, 2 * fb), BF),
        dma((nz,)), dma((nr,)), dma((nz,)), dma((nr,)),
        *[dma((nr, ny - 1))] * 4,
        *[dma((ny,))] * 8,
        *[dma((nx,))] * 8,
        *[dma((nx + 1,))] * 8,
        *[dma((nr, ny - 1))] * 4,
        dma((2, nz)), dma((2, nz)), dma((2,)), dma((2,)), dma((6,)),
    ]
    shape = jax.ShapeDtypeStruct
    results = (
        shape((tb, dc), BF),
        shape((tb, dc), BF),
        shape((db, fb), BF),
        shape((db, fb), BF),
        shape((ny * fb, dc), BF),
    )
    held = pl.pallas_call(
        functools.partial(kernel, dims),
        out_shape=results,
        in_specs=[hbm] * 5,
        out_specs=(hbm,) * 5,
        scratch_shapes=scratch,
        compiler_params=pltpu.CompilerParams(
            collective_id=0, has_side_effects=True, vmem_limit_bytes=60 * 2**20
        ),
        name="swiglu",
    )(tokens, out_grad, gate_weight, up_weight, down_weight)
    return pl.pallas_call(
        place,
        out_shape=results,
        in_specs=[pl.BlockSpec(memory_space=pltpu.VMEM)] * 5,
        out_specs=(hbm,) * 5,
        scratch_shapes=[dma((5,))],
        compiler_params=pltpu.CompilerParams(has_side_effects=True),
        name="place",
    )(*held)


def solution(mesh):
    nr, nc = mesh.shape["row"], mesh.shape["col"]
    dims = (nr // 2, nc // nr, nr)
    spec = P("row", "col")
    return jax.shard_map(
        functools.partial(local, dims),
        mesh=mesh,
        in_specs=(spec,) * 5,
        out_specs=(spec,) * 5,
        check_vma=False,
    )
```

```python
import functools

import jax
import jax.numpy as jnp
from jax import lax
from jax.experimental import pallas as pl
from jax.experimental.pallas import tpu as pltpu
from jax.sharding import PartitionSpec as P

MESH = pl.DeviceIdType.MESH
BF = jnp.bfloat16
F32 = jnp.float32


def nn(a, b):
    return lax.dot_general(a, b, (((1,), (0,)), ((), ())), preferred_element_type=F32)


def nt(a, b):
    return lax.dot_general(a, b, (((1,), (1,)), ((), ())), preferred_element_type=F32)


def tn(a, b):
    return lax.dot_general(a, b, (((0,), (0,)), ((), ())), preferred_element_type=F32)


def kernel(
    dims,
    tok_hbm, cot_hbm, gate_hbm, up_hbm, down_hbm,
    out_o, tg_o, gg_o, ug_o, dg_o,
    tok, cot, down, xg, gw, dp, hh, hg, mid, mid2,
    acc_a, ms_a, mr_a, xs_a, xr_a,
    acc_b, ms_b, mr_b, xs_b, xr_b,
    o32, os_o, own_o, yr_o, os_t, own_t, yr_t,
    zs, zr, zown, fs, dgs, wgs,
    tos, tor, cos, cor, tys, tyr, cys, cyr,
    d1s, d1r, d2s, d2r, e1s, e1r, e2s, e2r,
    mas, mar, mbs, mbr, xas, xar, xbs, xbr,
    hxs, hxr, hms, hmr, gxs, gxr, gms, gmr,
    yos, yor, yts, ytr, zsm, zrm, f_s, f_r, lsem,
):
    nx, ny, nz = dims
    nr = 2 * nx
    tb, dc = tok.shape
    db, fb = gate_hbm.shape

    row, col = lax.axis_index("row"), lax.axis_index("col")
    x, kap = lax.div(row, 2), lax.rem(row, 2)
    z, y = lax.div(col, ny), lax.rem(col, ny)
    mate = (x * 2 + 1 - kap, col)
    diag = row == z
    twin = (z, row * ny + y)

    near = sorted({1, nx - 1})
    opposite = nx // 2 if nx > 2 else 0

    near_y = sorted({1, ny - 1})
    far_y = ny // 2 if ny > 2 else 0

    def xdev(d):
        return (lax.rem(x + d, nx) * 2 + kap, col)

    def ydev(d):
        return (row, z * ny + lax.rem(y + d, ny))

    def zdev(d):
        return (row, lax.rem(z + d, nz) * ny + y)

    def panel_to(d):
        return (z, lax.rem(z + d, nz) * ny + y)

    def panel_from(r):
        return (r, row * ny + y)

    def leg1_to(k):
        return (lax.rem(x + y - k + 1 + nx, nx) * 2 + kap, z * ny + k)

    def leg1_from(s):
        return (lax.rem(x + y - s - 1 + 2 * nx, nx) * 2 + kap, z * ny + s)

    def leg2_to(s):
        return (z, (lax.rem(x + y - s - 1 + 2 * nx, nx) * 2 + kap) * ny + y)

    def leg2_from(s):
        return (lax.rem(lax.div(z, 2) + s - y + 1 + nx, nx) * 2 + lax.rem(z, 2), row * ny + y)

    def leg2_home(s):
        return jnp.logical_and(diag, lax.rem(x + y - s - 1 + 2 * nx, nx) == x)

    def leg2_kept(s):
        return jnp.logical_and(diag, lax.rem(x + s - y + 1 + nx, nx) == x)

    def rows(t):
        return pl.ds(pl.multiple_of(t * tb, tb), tb)

    def lanes(k):
        return pl.ds(pl.multiple_of(k * dc, dc), dc)

    def frows(k):
        return pl.ds(pl.multiple_of(k * fb, fb), fb)

    def rc(src, dst, ss, rs, dev):
        return pltpu.make_async_remote_copy(
            src_ref=src, dst_ref=dst, send_sem=ss, recv_sem=rs,
            device_id=dev, device_id_type=MESH,
        )

    def hcopy(buf, t, ss, rs, dev):
        return rc(buf.at[rows(t)], buf.at[rows(t)], ss, rs, dev)

    def hhalf(buf, t, way, ss, rs, dev):
        ht = tb // 2
        ref = buf.at[pl.ds(pl.multiple_of(t * tb + way * ht, ht), ht)]
        return rc(ref, ref, ss, rs, dev)

    def no(cond):
        return jnp.logical_not(cond)

    loads = [
        pltpu.make_async_copy(src, dst, lsem.at[i])
        for i, (src, dst) in enumerate((
            (tok_hbm, tok),
            (cot_hbm, cot),
            (down_hbm, down),
            (gate_hbm, gw.at[:, pl.ds(0, fb)]),
            (up_hbm, gw.at[:, pl.ds(fb, fb)]),
        ))
    ]
    for load in loads:
        load.start()

    bar = pltpu.get_barrier_semaphore()

    def greet(dev):
        pl.semaphore_signal(bar, inc=1, device_id=dev, device_id_type=MESH)

    greet(mate)
    for d in range(1, nx):
        greet(xdev(d))
    for d in range(1, ny):
        greet(ydev(d))
    for d in range(1, nz):
        greet(zdev(d))

    count = 1 + (nx - 1) + (ny - 1) + (nz - 1) + 2 * ny
    for d in range(nz):
        @pl.when(no(jnp.logical_and(diag, d == 0)))
        def _():
            greet(panel_to(d))

        @pl.when(no(jnp.logical_and(diag, row == d)))
        def _():
            greet(panel_from(d))

        count = count + jnp.where(jnp.logical_and(diag, d == 0), 0, 1)
        count = count + jnp.where(jnp.logical_and(diag, row == d), 0, 1)
    for s in range(ny):
        greet(leg1_to(s))
        greet(leg1_from(s))

        @pl.when(no(leg2_home(s)))
        def _():
            greet(leg2_to(s))

        @pl.when(no(leg2_kept(s)))
        def _():
            greet(leg2_from(s))

        count = count + jnp.where(leg2_home(s), 0, 1) + jnp.where(leg2_kept(s), 0, 1)
    pl.semaphore_wait(bar, count)

    def sub(w, k):
        return lanes(w * ny + k)

    far_first = sorted(range(nz), key=lambda d: -min(d, nz - d))

    def panel_send(w):
        src, ss, sr = ((tok, tos, tor), (cot, cos, cor))[w]
        for d in far_first:
            @pl.when(no(jnp.logical_and(diag, d == 0)))
            def _():
                rc(src, xg.at[rows(row), sub(w, y)], ss.at[d], sr.at[row], panel_to(d)).start()

        @pl.when(diag)
        def _():
            xg[rows(row), sub(w, y)] = src[...]

    def panel_y(w, r, d):
        ss, sr = ((tys, tyr), (cys, cyr))[w]
        ref = xg.at[rows(r), sub(w, y)]
        return rc(ref, ref, ss.at[r, d - 1], sr.at[r, d - 1], ydev(d))

    def panel_pass(w, r):
        sr = (tor, cor)[w]

        @pl.when(no(jnp.logical_and(diag, row == r)))
        def _():
            ref = xg.at[rows(r), sub(w, y)]
            rc(ref, ref, sr.at[r], sr.at[r], panel_from(r)).wait_recv()

        for d in near_y:
            panel_y(w, r, d).start()

    def panel_from_y(w, r, d, dev):
        ss, sr = ((tys, tyr), (cys, cyr))[w]
        ref = xg.at[rows(r), sub(w, lax.rem(y - d + ny, ny))]
        return rc(ref, ref, ss.at[r, d - 1], sr.at[r, d - 1], dev)

    def panel_next(w, r):
        for d in near_y:
            panel_from_y(w, r, d, ydev(d)).wait_recv()
        if far_y:
            sr = (tyr, cyr)[w]
            ss = (tys, cys)[w]
            for side, d in enumerate(near_y):
                @pl.when(lax.rem(r, 2) == side)
                def _():
                    ref = xg.at[rows(r), sub(w, lax.rem(y - d + ny, ny))]
                    rc(ref, ref, ss.at[r, far_y - 1], sr.at[r, far_y - 1], ydev(d)).start()

    def panel_whole(w, r):
        if far_y:
            panel_from_y(w, r, far_y, ydev(1)).wait_recv()

    def order(i):
        return lax.rem(x + 1 + lax.div(i, 2), nx) * 2 + lax.rem(i, 2)

    def leg2(src, dst_of, s1, r1, s2, r2, s):
        ref = src.at[s]
        rc(ref, ref, s1.at[s], r1.at[s], leg1_from(s)).wait_recv()

        @pl.when(no(leg2_home(s)))
        def _():
            rc(ref, dst_of(s), s2.at[s], r2.at[s], leg2_to(s)).start()

        @pl.when(leg2_home(s))
        def _():
            pltpu.make_async_copy(ref, dst_of(s), lsem.at[5]).start()
            pltpu.make_async_copy(ref, dst_of(s), lsem.at[5]).wait()

    def dp_at(s):
        return dp.at[:, lanes(s)]

    def dg_at(s):
        return dg_o.at[frows(s)]

    loads[2].wait()
    for k in range(ny):
        rc(down.at[frows(k)], mid.at[y], d1s.at[k], d1r.at[y], leg1_to(k)).start()

    loads[0].wait()
    panel_send(0)
    loads[1].wait()
    panel_send(1)

    def pass_tok(i, carry):
        panel_pass(0, order(i))
        return carry

    lax.fori_loop(0, nr, pass_tok, 0)
    loads[3].wait()
    loads[4].wait()

    def reduce_pair(t, acc, mr, xs, xr, ms_sem, mr_sem, xs_sem, xr_sem):
        xt = lax.div(t, 2)
        ref = mr.at[xt]
        rc(ref, ref, ms_sem.at[xt], mr_sem.at[xt], mate).wait_recv()

        @pl.when(xt == x)
        def _():
            acc[xt] = acc[xt] + mr[xt]

        @pl.when(xt != x)
        def _():
            d = lax.rem(xt - x + nx, nx)
            xs[d] = (acc[xt] + mr[xt]).astype(BF)
            rc(xs.at[d], xr.at[d], xs_sem.at[d], xr_sem.at[d], xdev(d)).start()

    set_a = (acc_a, mr_a, xs_a, xr_a, mas, mar, xas, xar)
    set_b = (acc_b, mr_b, xs_b, xr_b, mbs, mbr, xbs, xbr)

    def give(t, part, acc, ms, mr, s_sem, r_sem):
        xt = lax.div(t, 2)

        @pl.when(lax.rem(t, 2) == kap)
        def _():
            acc[xt] = part

        @pl.when(lax.rem(t, 2) != kap)
        def _():
            ms[xt] = part
            rc(ms.at[xt], mr.at[xt], s_sem.at[xt], r_sem.at[xt], mate).start()

    for s in range(ny):
        leg2(mid, dp_at, d1s, d1r, d2s, d2r, s)

    ahead = 2
    for i in range(ahead):
        panel_next(0, order(i))

    def step_a(i, carry):
        t = order(i)

        @pl.when(i + ahead < nr)
        def _():
            panel_next(0, order(i + ahead))

        panel_whole(0, t)
        part = nn(xg[rows(t), pl.ds(0, db)], gw[...])
        give(t, part, acc_a, ms_a, mr_a, mas, mar)

        before = order(jnp.maximum(i - 1, 0))

        @pl.when(jnp.logical_and(i > 0, lax.rem(before, 2) == kap))
        def _():
            reduce_pair(before, *set_a)

        @pl.when(i >= nr // 2)
        def _():
            panel_pass(1, order(2 * i - nr))
            panel_pass(1, order(2 * i - nr + 1))

        return carry

    lax.fori_loop(0, nr, step_a, 0)

    @pl.when(lax.rem(order(nr - 1), 2) == kap)
    def _():
        reduce_pair(order(nr - 1), *set_a)

    def next_cot(i, carry):
        panel_next(1, order(i))
        return carry

    lax.fori_loop(0, nr, next_cot, 0)

    chunk = 16

    def spot(i):
        r0 = pl.multiple_of(i * chunk, chunk)
        return pl.ds(r0, chunk), pl.ds(pl.multiple_of(row * tb + r0, chunk), chunk)

    for d in range(1, nx):
        rc(xr_a.at[d], xr_a.at[d], xas.at[d], xar.at[d], xdev(d)).wait_recv()

    def point_h(i, carry):
        here, there = spot(i)
        sa = acc_a[x, here, :]
        for d in range(1, nx):
            sa = sa + xr_a[d, here, :].astype(F32)
        acc_a[x, here, :] = sa
        g, u = sa[:, :fb], sa[:, fb:]
        hh[there, :] = (g * jax.nn.sigmoid(g) * u).astype(BF)
        return carry

    lax.fori_loop(0, tb // chunk, point_h, 0)

    def share(buf, xs_sem, xr_sem, ms_sem, mr_sem):
        for d in near:
            hcopy(buf, row, xs_sem.at[d], xr_sem.at[d], xdev(d)).start()
        hcopy(buf, row, ms_sem.at[0], mr_sem.at[0], mate).start()

    def kin(d):
        return lax.rem(x - d + nx, nx) * 2 + kap

    share(hh, hxs, hxr, hms, hmr)

    for s in range(ny):
        @pl.when(no(leg2_kept(s)))
        def _():
            rc(dp_at(s), dp_at(s), d2s.at[s], d2r.at[s], leg2_from(s)).wait_recv()

    def step_b(i, carry):
        t = order(i)
        panel_whole(1, t)
        part = nt(xg[rows(t), pl.ds(db, db)], dp[...])
        give(t, part, acc_b, ms_b, mr_b, mbs, mbr)

        before = order(jnp.maximum(i - 1, 0))

        @pl.when(jnp.logical_and(i > 0, lax.rem(before, 2) == kap))
        def _():
            reduce_pair(before, *set_b)

        return carry

    lax.fori_loop(0, nr, step_b, 0)

    @pl.when(lax.rem(order(nr - 1), 2) == kap)
    def _():
        reduce_pair(order(nr - 1), *set_b)

    def dist(j):
        q = lax.div(j, 2)
        return jnp.where(lax.rem(q, 2) == 1, lax.div(q + 1, 2), lax.rem(nx - lax.div(q, 2), nx))

    def block(j):
        src = lax.rem(x - dist(j) + nx, nx)
        return src * 2 + jnp.where(lax.rem(j, 2) == 0, kap, 1 - kap)

    def arrive(buf, j, xs_sem, xr_sem, ms_sem, mr_sem):
        t, d = block(j), dist(j)
        even = lax.rem(j, 2) == 0

        @pl.when(j == 2)
        def _():
            for e in near:
                hcopy(buf, kin(e), xs_sem.at[e], xr_sem.at[e], xdev(e)).wait_recv()
                if opposite:
                    way = 0 if e == 1 else 1
                    hhalf(buf, kin(e), way, xs_sem.at[2 + way * (nx - 2)], xr_sem.at[2 + way * (nx - 2)], xdev(e)).start()
            for e in near:
                hcopy(buf, kin(e), ms_sem.at[e], mr_sem.at[e], mate).start()

        if opposite:
            @pl.when(jnp.logical_and(even, d == opposite))
            def _():
                for way in range(2):
                    sem = xr_sem.at[2 + way * (nx - 2)]
                    hhalf(buf, t, way, sem, sem, xdev(1)).wait_recv()
                hcopy(buf, t, ms_sem.at[d], mr_sem.at[d], mate).start()

        @pl.when(no(even))
        def _():
            hcopy(buf, t, ms_sem.at[d], mr_sem.at[d], mate).wait_recv()

    def ycopy(w, t, d):
        os, yr, ss, rs = ((os_o, yr_o, yos, yor), (os_t, yr_t, yts, ytr))[w]
        return rc(os.at[t, d - 1], yr.at[t, d - 1], ss.at[t, d - 1], rs.at[t, d - 1], ydev(d))

    def spread(w, t, part):
        os, own = ((os_o, own_o), (os_t, own_t))[w]
        o32[...] = part
        for e in range(1, ny):
            os[t, e - 1] = o32[:, lanes(lax.rem(y + e, ny))].astype(BF)
            ycopy(w, t, e).start()
        own[t] = o32[:, lanes(y)]

    def zcopy(w, d):
        return rc(zs.at[w, d], zr.at[w, d], zsm.at[w, d], zrm.at[w, d], zdev(d))

    def reduce_y(w, t):
        own, yr = ((own_o, yr_o), (own_t, yr_t))[w]
        total = own[t]
        for d in range(1, ny):
            ycopy(w, t, d).wait_recv()
            total = total + yr[t, d - 1].astype(F32)

        @pl.when(t == z)
        def _():
            zown[w] = total

        @pl.when(t != z)
        def _():
            d = lax.rem(t - z + nz, nz)
            zs[w, d] = total.astype(BF)
            zcopy(w, d).start()

    def step_c(j, carry):
        arrive(hh, j, hxs, hxr, hms, hmr)
        t = block(j)
        spread(0, t, nn(hh[rows(t), :], dp[...]))
        return carry

    lax.fori_loop(0, nr, step_c, 0)

    for k in range(ny):
        dgs[k] = tn(hh[...], xg[:, pl.ds(db + k * dc, dc)]).astype(BF)
        rc(dgs.at[k], mid2.at[y], e1s.at[k], e1r.at[y], leg1_to(k)).start()

    for d in range(1, nx):
        rc(xr_b.at[d], xr_b.at[d], xbs.at[d], xbr.at[d], xdev(d)).wait_recv()

    def point_g(i, carry):
        here, there = spot(i)
        sa = acc_a[x, here, :]
        sb = acc_b[x, here, :]
        for d in range(1, nx):
            sb = sb + xr_b[d, here, :].astype(F32)
        g, u = sa[:, :fb], sa[:, fb:]
        sig = jax.nn.sigmoid(g)
        hg[there, pl.ds(0, fb)] = (sb * u * sig * (1.0 + g * (1.0 - sig))).astype(BF)
        hg[there, pl.ds(fb, fb)] = (sb * (g * sig)).astype(BF)
        return carry

    lax.fori_loop(0, tb // chunk, point_g, 0)
    share(hg, gxs, gxr, gms, gmr)

    def sum_o(j, carry):
        reduce_y(0, block(j))
        return carry

    lax.fori_loop(0, nr, sum_o, 0)

    for s in range(ny):
        leg2(mid2, dg_at, e1s, e1r, e2s, e2r, s)

    lag = 2

    def step_d(j, carry):
        arrive(hg, j, gxs, gxr, gms, gmr)
        t = block(j)
        spread(1, t, nt(hg[rows(t), :], gw[...]))
        @pl.when(j >= lag)
        def _():
            reduce_y(1, block(jnp.maximum(j - lag, 0)))

        return carry

    lax.fori_loop(0, nr, step_d, 0)

    for j in range(nr - lag, nr):
        reduce_y(1, block(j))

    for k in range(ny):
        w = tn(xg[:, pl.ds(k * dc, dc)], hg[...]).astype(BF)
        wgs[pl.ds(k * dc, dc)] = w

    grads = [
        pltpu.make_async_copy(wgs.at[:, pl.ds(i * fb, fb)], dst, lsem.at[i])
        for i, dst in enumerate((gg_o, ug_o))
    ]
    for copy in grads:
        copy.start()

    def fcopy(w):
        return rc(fs.at[w], (out_o, tg_o)[w], f_s.at[w], f_r.at[w], twin)

    for w in range(2):
        total = zown[w]
        for d in range(1, nz):
            zcopy(w, d).wait_recv()
            total = total + zr[w, d].astype(F32)
        fs[w] = total.astype(BF)

        @pl.when(diag)
        def _():
            kept = pltpu.make_async_copy(fs.at[w], (out_o, tg_o)[w], lsem.at[5])
            kept.start()
            kept.wait()

        @pl.when(no(diag))
        def _():
            fcopy(w).start()

    @pl.when(no(diag))
    def _():
        for w in range(2):
            fcopy(w).wait_recv()

    for s in range(ny):
        @pl.when(no(leg2_kept(s)))
        def _():
            rc(dg_at(s), dg_at(s), e2s.at[s], e2r.at[s], leg2_from(s)).wait_recv()

    for copy in grads:
        copy.wait()

    @pl.when(no(diag))
    def _():
        for w in range(2):
            fcopy(w).wait_send()

    for k in range(ny):
        rc(dgs.at[k], mid.at[k], d1s.at[k], d1r.at[k], leg1_to(k)).wait_send()
        rc(dgs.at[k], mid.at[k], e1s.at[k], e1r.at[k], leg1_to(k)).wait_send()

        @pl.when(no(leg2_home(k)))
        def _():
            rc(mid.at[k], dp_at(k), d2s.at[k], d2r.at[k], leg2_to(k)).wait_send()
            rc(mid2.at[k], dg_at(k), e2s.at[k], e2r.at[k], leg2_to(k)).wait_send()

    for d in range(nz):
        @pl.when(no(jnp.logical_and(diag, d == 0)))
        def _():
            rc(tok, tok, tos.at[d], tor.at[d], panel_to(d)).wait_send()
            rc(cot, cot, cos.at[d], cor.at[d], panel_to(d)).wait_send()

    for q in range(nx):
        rc(ms_a.at[q], mr_a.at[q], mas.at[q], mar.at[q], mate).wait_send()
        rc(ms_b.at[q], mr_b.at[q], mbs.at[q], mbr.at[q], mate).wait_send()
        hcopy(hh, row, hms.at[q], hmr.at[q], mate).wait_send()
        hcopy(hg, row, gms.at[q], gmr.at[q], mate).wait_send()
    for d in range(1, nx):
        rc(xs_a.at[d], xr_a.at[d], xas.at[d], xar.at[d], xdev(d)).wait_send()
        rc(xs_b.at[d], xr_b.at[d], xbs.at[d], xbr.at[d], xdev(d)).wait_send()
    for d in near:
        hcopy(hh, row, hxs.at[d], hxr.at[d], xdev(d)).wait_send()
        hcopy(hg, row, gxs.at[d], gxr.at[d], xdev(d)).wait_send()
    if opposite:
        for e in (2, nx):
            hhalf(hh, row, 0, hxs.at[e], hxr.at[e], xdev(1)).wait_send()
            hhalf(hg, row, 0, gxs.at[e], gxr.at[e], xdev(1)).wait_send()
    for d in range(1, nz):
        zcopy(0, d).wait_send()
        zcopy(1, d).wait_send()

    def ydone(t, carry):
        for d in range(1, ny):
            panel_y(0, t, d).wait_send()
            panel_y(1, t, d).wait_send()
            ycopy(0, t, d).wait_send()
            ycopy(1, t, d).wait_send()
        return carry

    lax.fori_loop(0, nr, ydone, 0)


def place(*refs):
    sems = refs[-1]
    copies = [
        pltpu.make_async_copy(src, dst, sems.at[i])
        for i, (src, dst) in enumerate(zip(refs[:5], refs[5:10]))
    ]
    for copy in copies:
        copy.start()
    for copy in copies:
        copy.wait()


def local(dims, tokens, gate_weight, up_weight, down_weight, out_grad):
    nx, ny, nz = dims
    nr = 2 * nx
    tb, dc = tokens.shape
    db, fb = gate_weight.shape
    t = nr * tb
    hbm = pl.BlockSpec(memory_space=pl.ANY)
    dma = pltpu.SemaphoreType.DMA

    def sums(width):
        return [
            pltpu.VMEM((nx, tb, width), F32),
            pltpu.VMEM((nx, tb, width), F32),
            pltpu.VMEM((nx, tb, width), F32),
            pltpu.VMEM((nx, tb, width), BF),
            pltpu.VMEM((nx, tb, width), BF),
        ]

    def shares():
        return [
            pltpu.VMEM((nr, ny - 1, tb, dc), BF),
            pltpu.VMEM((nr, tb, dc), F32),
            pltpu.VMEM((nr, ny - 1, tb, dc), BF),
        ]

    scratch = [
        pltpu.VMEM((tb, dc), BF),
        pltpu.VMEM((tb, dc), BF),
        pltpu.VMEM((ny * fb, dc), BF),
        pltpu.VMEM((t, 2 * db), BF),
        pltpu.VMEM((db, 2 * fb), BF),
        pltpu.VMEM((fb, db), BF),
        pltpu.VMEM((t, fb), BF),
        pltpu.VMEM((t, 2 * fb), BF),
        pltpu.VMEM((ny, fb, dc), BF),
        pltpu.VMEM((ny, fb, dc), BF),
        *sums(2 * fb),
        *sums(fb),
        pltpu.VMEM((tb, db), F32),
        *shares(),
        *shares(),
        pltpu.VMEM((2, nz, tb, dc), BF),
        pltpu.VMEM((2, nz, tb, dc), BF),
        pltpu.VMEM((2, tb, dc), F32),
        pltpu.VMEM((2, tb, dc), BF),
        pltpu.VMEM((ny, fb, dc), BF),
        pltpu.VMEM((db, 2 * fb), BF),
        dma((nz,)), dma((nr,)), dma((nz,)), dma((nr,)),
        *[dma((nr, ny - 1))] * 4,
        *[dma((ny,))] * 8,
        *[dma((nx,))] * 8,
        *[dma((nx + 1,))] * 8,
        *[dma((nr, ny - 1))] * 4,
        dma((2, nz)), dma((2, nz)), dma((2,)), dma((2,)), dma((6,)),
    ]
    shape = jax.ShapeDtypeStruct
    results = (
        shape((tb, dc), BF),
        shape((tb, dc), BF),
        shape((db, fb), BF),
        shape((db, fb), BF),
        shape((ny * fb, dc), BF),
    )
    held = pl.pallas_call(
        functools.partial(kernel, dims),
        out_shape=results,
        in_specs=[hbm] * 5,
        out_specs=(hbm,) * 5,
        scratch_shapes=scratch,
        compiler_params=pltpu.CompilerParams(
            collective_id=0, has_side_effects=True, vmem_limit_bytes=60 * 2**20
        ),
        name="swiglu",
    )(tokens, out_grad, gate_weight, up_weight, down_weight)
    return pl.pallas_call(
        place,
        out_shape=results,
        in_specs=[pl.BlockSpec(memory_space=pltpu.VMEM)] * 5,
        out_specs=(hbm,) * 5,
        scratch_shapes=[dma((5,))],
        compiler_params=pltpu.CompilerParams(has_side_effects=True),
        name="place",
    )(*held)


def solution(mesh):
    nr, nc = mesh.shape["row"], mesh.shape["col"]
    dims = (nr // 2, nc // nr, nr)
    spec = P("row", "col")
    return jax.shard_map(
        functools.partial(local, dims),
        mesh=mesh,
        in_specs=(spec,) * 5,
        out_specs=(spec,) * 5,
        check_vma=False,
    )
```

```python
import functools

import jax
import jax.numpy as jnp
from jax import lax
from jax.experimental import pallas as pl
from jax.experimental.pallas import tpu as pltpu
from jax.sharding import PartitionSpec as P

MESH = pl.DeviceIdType.MESH
BF = jnp.bfloat16
F32 = jnp.float32


def nn(a, b):
    return lax.dot_general(a, b, (((1,), (0,)), ((), ())), preferred_element_type=F32)


def nt(a, b):
    return lax.dot_general(a, b, (((1,), (1,)), ((), ())), preferred_element_type=F32)


def tn(a, b):
    return lax.dot_general(a, b, (((0,), (0,)), ((), ())), preferred_element_type=F32)


def kernel(
    dims,
    tok_hbm, cot_hbm, gate_hbm, up_hbm, down_hbm,
    out_o, tg_o, gg_o, ug_o, dg_o,
    tok, cot, down, xg, gw, dp, hh, hg, mid, mid2,
    acc_a, ms_a, mr_a, xs_a, xr_a,
    acc_b, ms_b, mr_b, xs_b, xr_b,
    o32, os_o, own_o, yr_o, os_t, own_t, yr_t,
    zs, zr, zown, fs, dgs, wgs,
    tos, tor, cos, cor, tys, tyr, cys, cyr,
    d1s, d1r, d2s, d2r, e1s, e1r, e2s, e2r,
    mas, mar, mbs, mbr, xas, xar, xbs, xbr,
    hxs, hxr, hms, hmr, gxs, gxr, gms, gmr,
    yos, yor, yts, ytr, zsm, zrm, f_s, f_r, lsem,
):
    nx, ny, nz = dims
    nr = 2 * nx
    tb, dc = tok.shape
    db, fb = gate_hbm.shape

    row, col = lax.axis_index("row"), lax.axis_index("col")
    x, kap = lax.div(row, 2), lax.rem(row, 2)
    z, y = lax.div(col, ny), lax.rem(col, ny)
    mate = (x * 2 + 1 - kap, col)
    diag = row == z
    twin = (z, row * ny + y)

    near = list(range(1, nx))

    near_y = sorted({1, ny - 1})
    far_y = ny // 2 if ny > 2 else 0

    def xdev(d):
        return (lax.rem(x + d, nx) * 2 + kap, col)

    def ydev(d):
        return (row, z * ny + lax.rem(y + d, ny))

    def zdev(d):
        return (row, lax.rem(z + d, nz) * ny + y)

    def panel_to(d):
        return (z, lax.rem(z + d, nz) * ny + y)

    def panel_from(r):
        return (r, row * ny + y)

    def leg1_to(k):
        return (lax.rem(x + y - k + 1 + nx, nx) * 2 + kap, z * ny + k)

    def leg1_from(s):
        return (lax.rem(x + y - s - 1 + 2 * nx, nx) * 2 + kap, z * ny + s)

    def leg2_to(s):
        return (z, (lax.rem(x + y - s - 1 + 2 * nx, nx) * 2 + kap) * ny + y)

    def leg2_from(s):
        return (lax.rem(lax.div(z, 2) + s - y + 1 + nx, nx) * 2 + lax.rem(z, 2), row * ny + y)

    def leg2_home(s):
        return jnp.logical_and(diag, lax.rem(x + y - s - 1 + 2 * nx, nx) == x)

    def leg2_kept(s):
        return jnp.logical_and(diag, lax.rem(x + s - y + 1 + nx, nx) == x)

    def rows(t):
        return pl.ds(pl.multiple_of(t * tb, tb), tb)

    def lanes(k):
        return pl.ds(pl.multiple_of(k * dc, dc), dc)

    def frows(k):
        return pl.ds(pl.multiple_of(k * fb, fb), fb)

    def rc(src, dst, ss, rs, dev):
        return pltpu.make_async_remote_copy(
            src_ref=src, dst_ref=dst, send_sem=ss, recv_sem=rs,
            device_id=dev, device_id_type=MESH,
        )

    def hcopy(buf, t, ss, rs, dev):
        return rc(buf.at[rows(t)], buf.at[rows(t)], ss, rs, dev)

    def no(cond):
        return jnp.logical_not(cond)

    loads = [
        pltpu.make_async_copy(src, dst, lsem.at[i])
        for i, (src, dst) in enumerate((
            (tok_hbm, tok),
            (cot_hbm, cot),
            (down_hbm, down),
            (gate_hbm, gw.at[:, pl.ds(0, fb)]),
            (up_hbm, gw.at[:, pl.ds(fb, fb)]),
        ))
    ]
    for load in loads:
        load.start()

    bar = pltpu.get_barrier_semaphore()

    def greet(dev):
        pl.semaphore_signal(bar, inc=1, device_id=dev, device_id_type=MESH)

    greet(mate)
    for d in range(1, nx):
        greet(xdev(d))
    for d in range(1, ny):
        greet(ydev(d))
    for d in range(1, nz):
        greet(zdev(d))

    count = 1 + (nx - 1) + (ny - 1) + (nz - 1) + 2 * ny
    for d in range(nz):
        @pl.when(no(jnp.logical_and(diag, d == 0)))
        def _():
            greet(panel_to(d))

        @pl.when(no(jnp.logical_and(diag, row == d)))
        def _():
            greet(panel_from(d))

        count = count + jnp.where(jnp.logical_and(diag, d == 0), 0, 1)
        count = count + jnp.where(jnp.logical_and(diag, row == d), 0, 1)
    for s in range(ny):
        greet(leg1_to(s))
        greet(leg1_from(s))

        @pl.when(no(leg2_home(s)))
        def _():
            greet(leg2_to(s))

        @pl.when(no(leg2_kept(s)))
        def _():
            greet(leg2_from(s))

        count = count + jnp.where(leg2_home(s), 0, 1) + jnp.where(leg2_kept(s), 0, 1)
    pl.semaphore_wait(bar, count)

    def sub(w, k):
        return lanes(w * ny + k)

    far_first = sorted(range(nz), key=lambda d: -min(d, nz - d))

    def panel_send(w):
        src, ss, sr = ((tok, tos, tor), (cot, cos, cor))[w]
        for d in far_first:
            @pl.when(no(jnp.logical_and(diag, d == 0)))
            def _():
                rc(src, xg.at[rows(row), sub(w, y)], ss.at[d], sr.at[row], panel_to(d)).start()

        @pl.when(diag)
        def _():
            xg[rows(row), sub(w, y)] = src[...]

    def panel_y(w, r, d):
        ss, sr = ((tys, tyr), (cys, cyr))[w]
        ref = xg.at[rows(r), sub(w, y)]
        return rc(ref, ref, ss.at[r, d - 1], sr.at[r, d - 1], ydev(d))

    def panel_pass(w, r):
        sr = (tor, cor)[w]

        @pl.when(no(jnp.logical_and(diag, row == r)))
        def _():
            ref = xg.at[rows(r), sub(w, y)]
            rc(ref, ref, sr.at[r], sr.at[r], panel_from(r)).wait_recv()

        for d in near_y:
            panel_y(w, r, d).start()

    def panel_from_y(w, r, d, dev):
        ss, sr = ((tys, tyr), (cys, cyr))[w]
        ref = xg.at[rows(r), sub(w, lax.rem(y - d + ny, ny))]
        return rc(ref, ref, ss.at[r, d - 1], sr.at[r, d - 1], dev)

    def panel_next(w, r):
        for d in near_y:
            panel_from_y(w, r, d, ydev(d)).wait_recv()
        if far_y:
            sr = (tyr, cyr)[w]
            ss = (tys, cys)[w]
            for side, d in enumerate(near_y):
                @pl.when(lax.rem(r, 2) == side)
                def _():
                    ref = xg.at[rows(r), sub(w, lax.rem(y - d + ny, ny))]
                    rc(ref, ref, ss.at[r, far_y - 1], sr.at[r, far_y - 1], ydev(d)).start()

    def panel_whole(w, r):
        if far_y:
            panel_from_y(w, r, far_y, ydev(1)).wait_recv()

    def order(i):
        return lax.rem(x + 1 + lax.div(i, 2), nx) * 2 + lax.rem(i, 2)

    def leg2(src, dst_of, s1, r1, s2, r2, s):
        ref = src.at[s]
        rc(ref, ref, s1.at[s], r1.at[s], leg1_from(s)).wait_recv()

        @pl.when(no(leg2_home(s)))
        def _():
            rc(ref, dst_of(s), s2.at[s], r2.at[s], leg2_to(s)).start()

        @pl.when(leg2_home(s))
        def _():
            pltpu.make_async_copy(ref, dst_of(s), lsem.at[5]).start()
            pltpu.make_async_copy(ref, dst_of(s), lsem.at[5]).wait()

    def dp_at(s):
        return dp.at[:, lanes(s)]

    def dg_at(s):
        return dg_o.at[frows(s)]

    loads[2].wait()
    for k in range(ny):
        rc(down.at[frows(k)], mid.at[y], d1s.at[k], d1r.at[y], leg1_to(k)).start()

    loads[0].wait()
    panel_send(0)
    loads[1].wait()
    panel_send(1)

    def pass_tok(i, carry):
        panel_pass(0, order(i))
        return carry

    lax.fori_loop(0, nr, pass_tok, 0)
    loads[3].wait()
    loads[4].wait()

    def reduce_pair(t, acc, mr, xs, xr, ms_sem, mr_sem, xs_sem, xr_sem):
        xt = lax.div(t, 2)
        ref = mr.at[xt]
        rc(ref, ref, ms_sem.at[xt], mr_sem.at[xt], mate).wait_recv()

        @pl.when(xt == x)
        def _():
            acc[xt] = acc[xt] + mr[xt]

        @pl.when(xt != x)
        def _():
            d = lax.rem(xt - x + nx, nx)
            xs[d] = (acc[xt] + mr[xt]).astype(BF)
            rc(xs.at[d], xr.at[d], xs_sem.at[d], xr_sem.at[d], xdev(d)).start()

    set_a = (acc_a, mr_a, xs_a, xr_a, mas, mar, xas, xar)
    set_b = (acc_b, mr_b, xs_b, xr_b, mbs, mbr, xbs, xbr)

    def give(t, part, acc, ms, mr, s_sem, r_sem):
        xt = lax.div(t, 2)

        @pl.when(lax.rem(t, 2) == kap)
        def _():
            acc[xt] = part

        @pl.when(lax.rem(t, 2) != kap)
        def _():
            ms[xt] = part
            rc(ms.at[xt], mr.at[xt], s_sem.at[xt], r_sem.at[xt], mate).start()

    for s in range(ny):
        leg2(mid, dp_at, d1s, d1r, d2s, d2r, s)

    ahead = 2
    for i in range(ahead):
        panel_next(0, order(i))

    def step_a(i, carry):
        t = order(i)

        @pl.when(i + ahead < nr)
        def _():
            panel_next(0, order(i + ahead))

        panel_whole(0, t)
        part = nn(xg[rows(t), pl.ds(0, db)], gw[...])
        give(t, part, acc_a, ms_a, mr_a, mas, mar)

        before = order(jnp.maximum(i - 1, 0))

        @pl.when(jnp.logical_and(i > 0, lax.rem(before, 2) == kap))
        def _():
            reduce_pair(before, *set_a)

        @pl.when(i >= nr // 2)
        def _():
            panel_pass(1, order(2 * i - nr))
            panel_pass(1, order(2 * i - nr + 1))

        return carry

    lax.fori_loop(0, nr, step_a, 0)

    @pl.when(lax.rem(order(nr - 1), 2) == kap)
    def _():
        reduce_pair(order(nr - 1), *set_a)

    def next_cot(i, carry):
        panel_next(1, order(i))
        return carry

    lax.fori_loop(0, nr, next_cot, 0)

    chunk = 16

    def spot(i):
        r0 = pl.multiple_of(i * chunk, chunk)
        return pl.ds(r0, chunk), pl.ds(pl.multiple_of(row * tb + r0, chunk), chunk)

    for d in range(1, nx):
        rc(xr_a.at[d], xr_a.at[d], xas.at[d], xar.at[d], xdev(d)).wait_recv()

    def point_h(i, carry):
        here, there = spot(i)
        sa = acc_a[x, here, :]
        for d in range(1, nx):
            sa = sa + xr_a[d, here, :].astype(F32)
        acc_a[x, here, :] = sa
        g, u = sa[:, :fb], sa[:, fb:]
        hh[there, :] = (g * jax.nn.sigmoid(g) * u).astype(BF)
        return carry

    lax.fori_loop(0, tb // chunk, point_h, 0)

    def share(buf, xs_sem, xr_sem, ms_sem, mr_sem):
        for d in near:
            hcopy(buf, row, xs_sem.at[d], xr_sem.at[d], xdev(d)).start()
        hcopy(buf, row, ms_sem.at[0], mr_sem.at[0], mate).start()

    def kin(d):
        return lax.rem(x - d + nx, nx) * 2 + kap

    share(hh, hxs, hxr, hms, hmr)

    for s in range(ny):
        @pl.when(no(leg2_kept(s)))
        def _():
            rc(dp_at(s), dp_at(s), d2s.at[s], d2r.at[s], leg2_from(s)).wait_recv()

    def step_b(i, carry):
        t = order(i)
        panel_whole(1, t)
        part = nt(xg[rows(t), pl.ds(db, db)], dp[...])
        give(t, part, acc_b, ms_b, mr_b, mbs, mbr)

        before = order(jnp.maximum(i - 1, 0))

        @pl.when(jnp.logical_and(i > 0, lax.rem(before, 2) == kap))
        def _():
            reduce_pair(before, *set_b)

        return carry

    lax.fori_loop(0, nr, step_b, 0)

    @pl.when(lax.rem(order(nr - 1), 2) == kap)
    def _():
        reduce_pair(order(nr - 1), *set_b)

    def dist(j):
        q = lax.div(j, 2)
        return jnp.where(lax.rem(q, 2) == 1, lax.div(q + 1, 2), lax.rem(nx - lax.div(q, 2), nx))

    def block(j):
        src = lax.rem(x - dist(j) + nx, nx)
        return src * 2 + jnp.where(lax.rem(j, 2) == 0, kap, 1 - kap)

    def arrive(buf, j, xs_sem, xr_sem, ms_sem, mr_sem):
        t, d = block(j), dist(j)
        even = lax.rem(j, 2) == 0

        @pl.when(jnp.logical_and(even, d > 0))
        def _():
            hcopy(buf, t, xs_sem.at[d], xr_sem.at[d], xdev(d)).wait_recv()
            hcopy(buf, t, ms_sem.at[d], mr_sem.at[d], mate).start()

        @pl.when(no(even))
        def _():
            hcopy(buf, t, ms_sem.at[d], mr_sem.at[d], mate).wait_recv()

    def ycopy(w, t, d):
        os, yr, ss, rs = ((os_o, yr_o, yos, yor), (os_t, yr_t, yts, ytr))[w]
        return rc(os.at[t, d - 1], yr.at[t, d - 1], ss.at[t, d - 1], rs.at[t, d - 1], ydev(d))

    def spread(w, t, part):
        os, own = ((os_o, own_o), (os_t, own_t))[w]
        o32[...] = part
        for e in range(1, ny):
            os[t, e - 1] = o32[:, lanes(lax.rem(y + e, ny))].astype(BF)
            ycopy(w, t, e).start()
        own[t] = o32[:, lanes(y)]

    def zcopy(w, d):
        return rc(zs.at[w, d], zr.at[w, d], zsm.at[w, d], zrm.at[w, d], zdev(d))

    def reduce_y(w, t):
        own, yr = ((own_o, yr_o), (own_t, yr_t))[w]
        total = own[t]
        for d in range(1, ny):
            ycopy(w, t, d).wait_recv()
            total = total + yr[t, d - 1].astype(F32)

        @pl.when(t == z)
        def _():
            zown[w] = total

        @pl.when(t != z)
        def _():
            d = lax.rem(t - z + nz, nz)
            zs[w, d] = total.astype(BF)
            zcopy(w, d).start()

    def step_c(j, carry):
        arrive(hh, j, hxs, hxr, hms, hmr)
        t = block(j)
        spread(0, t, nn(hh[rows(t), :], dp[...]))
        return carry

    lax.fori_loop(0, nr, step_c, 0)

    for k in range(ny):
        dgs[k] = tn(hh[...], xg[:, pl.ds(db + k * dc, dc)]).astype(BF)
        rc(dgs.at[k], mid2.at[y], e1s.at[k], e1r.at[y], leg1_to(k)).start()

    for d in range(1, nx):
        rc(xr_b.at[d], xr_b.at[d], xbs.at[d], xbr.at[d], xdev(d)).wait_recv()

    def point_g(i, carry):
        here, there = spot(i)
        sa = acc_a[x, here, :]
        sb = acc_b[x, here, :]
        for d in range(1, nx):
            sb = sb + xr_b[d, here, :].astype(F32)
        g, u = sa[:, :fb], sa[:, fb:]
        sig = jax.nn.sigmoid(g)
        hg[there, pl.ds(0, fb)] = (sb * u * sig * (1.0 + g * (1.0 - sig))).astype(BF)
        hg[there, pl.ds(fb, fb)] = (sb * (g * sig)).astype(BF)
        return carry

    lax.fori_loop(0, tb // chunk, point_g, 0)
    share(hg, gxs, gxr, gms, gmr)

    def sum_o(j, carry):
        reduce_y(0, block(j))
        return carry

    lax.fori_loop(0, nr, sum_o, 0)

    for s in range(ny):
        leg2(mid2, dg_at, e1s, e1r, e2s, e2r, s)

    lag = 2

    def step_d(j, carry):
        arrive(hg, j, gxs, gxr, gms, gmr)
        t = block(j)
        spread(1, t, nt(hg[rows(t), :], gw[...]))
        @pl.when(j >= lag)
        def _():
            reduce_y(1, block(jnp.maximum(j - lag, 0)))

        return carry

    lax.fori_loop(0, nr, step_d, 0)

    for j in range(nr - lag, nr):
        reduce_y(1, block(j))

    for k in range(ny):
        w = tn(xg[:, pl.ds(k * dc, dc)], hg[...]).astype(BF)
        wgs[pl.ds(k * dc, dc)] = w

    grads = [
        pltpu.make_async_copy(wgs.at[:, pl.ds(i * fb, fb)], dst, lsem.at[i])
        for i, dst in enumerate((gg_o, ug_o))
    ]
    for copy in grads:
        copy.start()

    def fcopy(w):
        return rc(fs.at[w], (out_o, tg_o)[w], f_s.at[w], f_r.at[w], twin)

    for w in range(2):
        total = zown[w]
        for d in range(1, nz):
            zcopy(w, d).wait_recv()
            total = total + zr[w, d].astype(F32)
        fs[w] = total.astype(BF)

        @pl.when(diag)
        def _():
            kept = pltpu.make_async_copy(fs.at[w], (out_o, tg_o)[w], lsem.at[5])
            kept.start()
            kept.wait()

        @pl.when(no(diag))
        def _():
            fcopy(w).start()

    @pl.when(no(diag))
    def _():
        for w in range(2):
            fcopy(w).wait_recv()

    for s in range(ny):
        @pl.when(no(leg2_kept(s)))
        def _():
            rc(dg_at(s), dg_at(s), e2s.at[s], e2r.at[s], leg2_from(s)).wait_recv()

    for copy in grads:
        copy.wait()

    @pl.when(no(diag))
    def _():
        for w in range(2):
            fcopy(w).wait_send()

    for k in range(ny):
        rc(dgs.at[k], mid.at[k], d1s.at[k], d1r.at[k], leg1_to(k)).wait_send()
        rc(dgs.at[k], mid.at[k], e1s.at[k], e1r.at[k], leg1_to(k)).wait_send()

        @pl.when(no(leg2_home(k)))
        def _():
            rc(mid.at[k], dp_at(k), d2s.at[k], d2r.at[k], leg2_to(k)).wait_send()
            rc(mid2.at[k], dg_at(k), e2s.at[k], e2r.at[k], leg2_to(k)).wait_send()

    for d in range(nz):
        @pl.when(no(jnp.logical_and(diag, d == 0)))
        def _():
            rc(tok, tok, tos.at[d], tor.at[d], panel_to(d)).wait_send()
            rc(cot, cot, cos.at[d], cor.at[d], panel_to(d)).wait_send()

    for q in range(nx):
        rc(ms_a.at[q], mr_a.at[q], mas.at[q], mar.at[q], mate).wait_send()
        rc(ms_b.at[q], mr_b.at[q], mbs.at[q], mbr.at[q], mate).wait_send()
        hcopy(hh, row, hms.at[q], hmr.at[q], mate).wait_send()
        hcopy(hg, row, gms.at[q], gmr.at[q], mate).wait_send()
    for d in range(1, nx):
        rc(xs_a.at[d], xr_a.at[d], xas.at[d], xar.at[d], xdev(d)).wait_send()
        rc(xs_b.at[d], xr_b.at[d], xbs.at[d], xbr.at[d], xdev(d)).wait_send()
    for d in near:
        hcopy(hh, row, hxs.at[d], hxr.at[d], xdev(d)).wait_send()
        hcopy(hg, row, gxs.at[d], gxr.at[d], xdev(d)).wait_send()
    for d in range(1, nz):
        zcopy(0, d).wait_send()
        zcopy(1, d).wait_send()

    def ydone(t, carry):
        for d in range(1, ny):
            panel_y(0, t, d).wait_send()
            panel_y(1, t, d).wait_send()
            ycopy(0, t, d).wait_send()
            ycopy(1, t, d).wait_send()
        return carry

    lax.fori_loop(0, nr, ydone, 0)


def place(*refs):
    sems = refs[-1]
    copies = [
        pltpu.make_async_copy(src, dst, sems.at[i])
        for i, (src, dst) in enumerate(zip(refs[:5], refs[5:10]))
    ]
    for copy in copies:
        copy.start()
    for copy in copies:
        copy.wait()


def local(dims, tokens, gate_weight, up_weight, down_weight, out_grad):
    nx, ny, nz = dims
    nr = 2 * nx
    tb, dc = tokens.shape
    db, fb = gate_weight.shape
    t = nr * tb
    hbm = pl.BlockSpec(memory_space=pl.ANY)
    dma = pltpu.SemaphoreType.DMA

    def sums(width):
        return [
            pltpu.VMEM((nx, tb, width), F32),
            pltpu.VMEM((nx, tb, width), F32),
            pltpu.VMEM((nx, tb, width), F32),
            pltpu.VMEM((nx, tb, width), BF),
            pltpu.VMEM((nx, tb, width), BF),
        ]

    def shares():
        return [
            pltpu.VMEM((nr, ny - 1, tb, dc), BF),
            pltpu.VMEM((nr, tb, dc), F32),
            pltpu.VMEM((nr, ny - 1, tb, dc), BF),
        ]

    scratch = [
        pltpu.VMEM((tb, dc), BF),
        pltpu.VMEM((tb, dc), BF),
        pltpu.VMEM((ny * fb, dc), BF),
        pltpu.VMEM((t, 2 * db), BF),
        pltpu.VMEM((db, 2 * fb), BF),
        pltpu.VMEM((fb, db), BF),
        pltpu.VMEM((t, fb), BF),
        pltpu.VMEM((t, 2 * fb), BF),
        pltpu.VMEM((ny, fb, dc), BF),
        pltpu.VMEM((ny, fb, dc), BF),
        *sums(2 * fb),
        *sums(fb),
        pltpu.VMEM((tb, db), F32),
        *shares(),
        *shares(),
        pltpu.VMEM((2, nz, tb, dc), BF),
        pltpu.VMEM((2, nz, tb, dc), BF),
        pltpu.VMEM((2, tb, dc), F32),
        pltpu.VMEM((2, tb, dc), BF),
        pltpu.VMEM((ny, fb, dc), BF),
        pltpu.VMEM((db, 2 * fb), BF),
        dma((nz,)), dma((nr,)), dma((nz,)), dma((nr,)),
        *[dma((nr, ny - 1))] * 4,
        *[dma((ny,))] * 8,
        *[dma((nx,))] * 8,
        *[dma((nx + 1,))] * 8,
        *[dma((nr, ny - 1))] * 4,
        dma((2, nz)), dma((2, nz)), dma((2,)), dma((2,)), dma((6,)),
    ]
    shape = jax.ShapeDtypeStruct
    results = (
        shape((tb, dc), BF),
        shape((tb, dc), BF),
        shape((db, fb), BF),
        shape((db, fb), BF),
        shape((ny * fb, dc), BF),
    )
    held = pl.pallas_call(
        functools.partial(kernel, dims),
        out_shape=results,
        in_specs=[hbm] * 5,
        out_specs=(hbm,) * 5,
        scratch_shapes=scratch,
        compiler_params=pltpu.CompilerParams(
            collective_id=0, has_side_effects=True, vmem_limit_bytes=60 * 2**20
        ),
        name="swiglu",
    )(tokens, out_grad, gate_weight, up_weight, down_weight)
    return pl.pallas_call(
        place,
        out_shape=results,
        in_specs=[pl.BlockSpec(memory_space=pltpu.VMEM)] * 5,
        out_specs=(hbm,) * 5,
        scratch_shapes=[dma((5,))],
        compiler_params=pltpu.CompilerParams(has_side_effects=True),
        name="place",
    )(*held)


def solution(mesh):
    nr, nc = mesh.shape["row"], mesh.shape["col"]
    dims = (nr // 2, nc // nr, nr)
    spec = P("row", "col")
    return jax.shard_map(
        functools.partial(local, dims),
        mesh=mesh,
        in_specs=(spec,) * 5,
        out_specs=(spec,) * 5,
        check_vma=False,
    )
```
